128 devices in a mesh: iy: 4 (over z), ix: 2 (over core), gz: 16 (over x, y).
Axes of the slice: x: 4, y: 4, z: 4, core: 2. Of those that a mesh axis runs over, the one named last changes fastest.
Arguments:
- fields: float32 [2, 512, 512, 512], P(None, 'gz', 'iy', 'ix'), may hold values from -6 to 6
- palette: float32 [2, 3], replicated, may hold values from -2 to 2
Outputs:
- image: float32 [4, 512, 512], P(None, ('iy', 'gz'), 'ix')
The draws below stay inside these ranges and needn't reach their ends.
All inputs are finite; a program needn't handle non-finite values.
Results may differ from the reference program's by a relative error of at most 0.0003.
Values sent between devices are 32-bit elements; how exact they have to be, the bound alone decides.
A program may use at most 128 MiB of HBM per device.

```python
import jax
import jax.numpy as jnp
from jax import lax

NZ = 512
NY = 512
NX = 512


def steps_of(rng, dims, cuts, smallest, top_value):
    factor_of, own = 1.0, jax.random.fold_in(rng, 6)
    for position, shards_of in cuts:
        heights = jnp.exp(jax.random.uniform(jax.random.fold_in(own, position), (shards_of,), jnp.float32, smallest / len(cuts), top_value / len(cuts)))
        factor_of = factor_of * jnp.repeat(heights, dims[position] // shards_of).reshape([-1 if axis == position else 1 for axis in range(len(dims))])
    return factor_of


def bell_draw(stream_key, dims, deviation, reach, pieces=(), held_as=jnp.bfloat16):
    level = steps_of(stream_key, dims, pieces, -0.22, 0.18) if pieces else 1.0
    result = jax.random.normal(stream_key, dims, jnp.float32) * deviation * level
    return jnp.minimum(jnp.maximum(result, -reach), reach).astype(held_as)


def setup_inputs(seed: int = 0) -> dict:
    arg_keys = jax.random.split(jax.random.key(seed), 3)
    fields = bell_draw(arg_keys[0], (2, NZ, NY, NX), 1.0, 6.0, ((1, 16), (2, 4), (3, 2)), jnp.float32)
    palette = jnp.clip(jax.random.uniform(arg_keys[1], (2, 3), jnp.float32, -2.0, 2.0), -2.0, 2.0)
    return dict(fields=fields, palette=palette)


row_block = 8

def central(field):
    grad_z = 0.5 * (field[2:, 1:-1, 1:-1] - field[:-2, 1:-1, 1:-1])
    grad_y = 0.5 * (field[1:-1, 2:, 1:-1] - field[1:-1, :-2, 1:-1])
    grad_x = 0.5 * (field[1:-1, 1:-1, 2:] - field[1:-1, 1:-1, :-2])
    return (grad_z, grad_y, grad_x)

def shade(padded, palette):
    density = padded[0]
    heat = padded[1]
    grad_z, grad_y, grad_x = central(density)
    slope = grad_z * grad_z + grad_y * grad_y + grad_x * grad_x
    heat_z, heat_y, heat_x = central(heat)
    edges = heat_z * heat_z + heat_y * heat_y + heat_x * heat_x
    inner = density[1:-1, 1:-1, 1:-1]
    optical = 0.004 * jnp.exp(inner) * (0.25 + slope / (1.0 + slope))
    facing = jnp.abs(0.36 * grad_z + 0.48 * grad_y + 0.8 * grad_x) / jnp.sqrt(1.0 + slope)
    lighting = (0.3 + 0.7 * facing) * (0.5 + edges / (1.0 + edges))
    heat_inner = heat[1:-1, 1:-1, 1:-1]
    emitted = jax.nn.sigmoid(palette[0][:, None, None, None] * heat_inner[None] + palette[1][:, None, None, None]) * lighting[None]
    return (optical, emitted)

def render_rows(fields, palette, start):
    rows = jnp.clip(start - 1 + jnp.arange(row_block + 2, dtype=jnp.int32), 0, NY - 1).astype(jnp.int32)
    block = jnp.take(fields, rows, axis=2)
    block = jnp.pad(block, ((0, 0), (1, 1), (0, 0), (1, 1)), mode='edge')
    optical, emitted = shade(block, palette)
    before = jnp.cumsum(optical, axis=0) - optical
    weight = jnp.exp(-before) * (1.0 - jnp.exp(-optical))
    colors = lax.optimization_barrier(jnp.sum(weight[None] * emitted, axis=1))
    opacity = 1.0 - jnp.exp(-lax.optimization_barrier(jnp.sum(optical, axis=0)))
    return jnp.concatenate([colors, opacity[None]], axis=0)

def reference(fields, palette):
    starts = (jnp.arange(NY // row_block, dtype=jnp.int32) * row_block).astype(jnp.int32)
    blocks = lax.map(lambda start: render_rows(fields, palette, start), starts)
    return jnp.transpose(blocks, (1, 0, 2, 3)).reshape(4, NY, NX)
```

```python
import functools

import jax
import jax.numpy as jnp
from jax import lax
from jax.experimental import pallas as pl
from jax.experimental.pallas import tpu as pltpu
from jax.sharding import PartitionSpec as P

MESH = pl.DeviceIdType.MESH
F32 = jnp.float32
LANES = 128
ROWS = 8
LOG2E = 1.4426950408889634
C1 = 0.005 * LOG2E
C2 = 0.016 * LOG2E


def cell(dz, dy, dx, s, ez, ey, ex, u, pal, nz, ny):
    r = lax.rsqrt(dz * dz + dy * dy + dx * dx + 4.0)
    depth = jnp.exp2(s * LOG2E) * (C2 * (r * r) - C1)
    face = jnp.abs(nz * dz + ny * dy + dx) * r + 0.3 / 0.56
    around = pltpu.reciprocal(ez * ez + ey * ey + ex * ex + 4.0, approx=True)
    light = face * (0.375 - around)
    tints = [jnp.tanh(pal[0][c] * u + pal[1][c]) for c in range(3)]
    return depth, light, tints


def kernel(
    sizes, lag, lead, group,
    pal_ref, f_ref, o_ref,
    vol, zh, hs, hx, inner, part, recv,
    load_sem, zsend, zrecv, ysend, yrecv, xsend, xrecv, asend, arecv,
):
    n_iy, n_ix, n_gz = sizes
    nz, ny = f_ref.shape[1], f_ref.shape[2]
    nb = n_gz
    ng = nb // group
    iy, ix, g = lax.axis_index("iy"), lax.axis_index("ix"), lax.axis_index("gz")
    sgn = jnp.where(g < nb // 2, 1, -1)
    hh, hc = 1 - ix, ix
    top, bottom = ROWS - 1, ROWS + ny

    def wrap(i, n):
        return lax.rem(i + 2 * n, n)

    def order(i):
        return wrap(g + sgn * (i + 1), nb)

    def rows8(b):
        return pl.ds(pl.multiple_of(ROWS * b, ROWS), ROWS)

    def shifted(b, by):
        return pl.ds(pl.multiple_of(ROWS * b, ROWS) + by, ROWS)

    def load(l, half):
        b = wrap(g + sgn * l, nb)
        return pltpu.make_async_copy(
            f_ref.at[:, :, rows8(b), pl.ds(half * LANES, LANES)],
            vol.at[half, :, :, shifted(b, ROWS), :],
            load_sem.at[l, half],
        )

    def start_load(l, _):
        for half in range(2):
            load(l, half).start()
        return 0

    def wait_load(l):
        for half in range(2):
            load(l, half).wait()

    lax.fori_loop(0, nb, start_load, 0)

    barrier = pltpu.get_barrier_semaphore()

    def greet(j, _):
        pl.semaphore_signal(
            barrier, inc=1, device_id={"gz": wrap(g + j, nb)}, device_id_type=MESH
        )
        return 0

    lax.fori_loop(1, nb, greet, 0)
    pl.semaphore_signal(barrier, inc=1, device_id={"ix": 1 - ix}, device_id_type=MESH)

    @pl.when(iy > 0)
    def _():
        pl.semaphore_signal(barrier, inc=1, device_id={"iy": iy - 1}, device_id_type=MESH)

    @pl.when(iy < n_iy - 1)
    def _():
        pl.semaphore_signal(barrier, inc=1, device_id={"iy": iy + 1}, device_id_type=MESH)

    pl.semaphore_wait(barrier, nb + jnp.where(iy > 0, 1, 0) + jnp.where(iy < n_iy - 1, 1, 0))

    def y_copy(side, half, remote):
        source = 0 if remote == (side == 1) else ny - 1
        src = f_ref.at[:, :, pl.ds(source, 1), pl.ds(half * LANES, LANES)]
        dst = vol.at[half, :, :, pl.ds(bottom if side else top, 1), :]
        if not remote:
            return pltpu.make_async_copy(src, dst, yrecv.at[side, half])
        return pltpu.make_async_remote_copy(
            src, dst, ysend.at[side, half], yrecv.at[side, half],
            device_id={"iy": iy - 1 if side else iy + 1}, device_id_type=MESH,
        )

    def z_rows(q):
        n = ROWS * group
        return pl.ds(pl.multiple_of(q * n, n), n)

    def z_copy(side, q, remote):
        source = 0 if remote == (side == 1) else nz - 1
        src = f_ref.at[:, source, z_rows(q), :]
        dst = zh.at[side, :, z_rows(q), :]
        if not remote:
            return pltpu.make_async_copy(src, dst, zrecv.at[side, q])
        return pltpu.make_async_remote_copy(
            src, dst, zsend.at[side, q], zrecv.at[side, q],
            device_id={"gz": g - 1 if side else g + 1}, device_id_type=MESH,
        )

    def first_group(gg):
        sg = jnp.where(gg < nb // 2, 1, -1)
        return lax.div(wrap(gg + sg, nb), group), sg

    def z_start(j, _):
        @pl.when(g < nb - 1)
        def _():
            q0, sg = first_group(g + 1)
            z_copy(0, wrap(q0 + sg * j, ng), True).start()

        @pl.when(g > 0)
        def _():
            q0, sg = first_group(g - 1)
            z_copy(1, wrap(q0 + sg * j, ng), True).start()

        @pl.when(g == 0)
        def _():
            z_copy(0, j, False).start()

        @pl.when(g == nb - 1)
        def _():
            z_copy(1, j, False).start()

        return 0

    def y_start():
        for half in range(2):
            @pl.when(iy < n_iy - 1)
            def _():
                y_copy(0, half, True).start()

            @pl.when(iy > 0)
            def _():
                y_copy(1, half, True).start()

            @pl.when(iy == 0)
            def _():
                y_copy(0, half, False).start()

            @pl.when(iy == n_iy - 1)
            def _():
                y_copy(1, half, False).start()

    lane = lax.broadcasted_iota(jnp.int32, (ROWS, LANES), 1)
    out_roll = jnp.where(ix == 0, LANES - 1, 1)
    in_roll = LANES - out_roll
    edge = jnp.where(ix == 0, LANES - 1, 0)
    at_edge = lane == edge
    at_inner = lane == LANES - 1 - edge
    nz_dir = jnp.where(ix == 0, 0.45, -0.45).astype(F32)
    ny_dir = jnp.where(ix == 0, 0.6, -0.6).astype(F32)
    pal = [[0.5 * pal_ref[i, c] for c in range(3)] for i in range(2)]

    def pack(b):
        for f in range(2):
            acc = None
            for z in range(nz):
                column = pltpu.roll(
                    vol[hh, f, z, shifted(b, ROWS), :], lax.rem(z - edge + LANES, LANES), 1
                )
                acc = column if acc is None else jnp.where(lane == z, column, acc)
            hs[f, rows8(b), :] = acc

    def x_copy(b):
        return pltpu.make_async_remote_copy(
            hs.at[:, rows8(b), :], hx.at[:, rows8(b), :], xsend.at[b], xrecv.at[b],
            device_id={"ix": 1 - ix}, device_id_type=MESH,
        )

    def a_copy(b, slot):
        return pltpu.make_async_remote_copy(
            part.at[b], recv.at[slot], asend.at[b], arecv.at[slot],
            device_id={"gz": b}, device_id_type=MESH,
        )

    def planes(b, f, z):
        return [vol[half, f, z, shifted(b, ROWS), :] for half in (hc, hh)]

    def layer(b, z, before, now, after):
        diffs = []
        for f in range(2):
            c, h = now[f]
            beside = pltpu.roll(hx[f, rows8(b), :], lax.rem(edge - z + LANES, LANES), 1)
            oc, oh = pltpu.roll(c, out_roll, 1), pltpu.roll(h, out_roll, 1)
            ic, ih = pltpu.roll(c, in_roll, 1), pltpu.roll(h, in_roll, 1)
            dx = [
                jnp.where(at_edge, oh, oc) - jnp.where(at_inner, c, ic),
                jnp.where(at_edge, beside, oh) - jnp.where(at_inner, ic, ih),
            ]
            dy = [
                vol[half, f, z, shifted(b, ROWS + 1), :] - vol[half, f, z, shifted(b, ROWS - 1), :]
                for half in (hc, hh)
            ]
            dz = [after[f][k] - before[f][k] for k in range(2)]
            diffs.append((dz, dy, dx))
        (dz, dy, dx), (ez, ey, ex) = diffs
        return [
            cell(
                dz[k], dy[k], dx[k], now[0][k], ez[k], ey[k], ex[k], now[1][k],
                pal, nz_dir, ny_dir,
            )
            for k in range(2)
        ]

    def interior(b):
        zero, one = jnp.zeros((ROWS, LANES), F32), jnp.ones((ROWS, LANES), F32)
        depth, left = [zero, zero], [one, one]
        sums = [[zero] * 4, [zero] * 4]
        before = [planes(b, f, 0) for f in range(2)]
        now = [planes(b, f, 1) for f in range(2)]
        for z in range(1, nz - 1):
            after = [planes(b, f, z + 1) for f in range(2)]
            for k, (d, light, tints) in enumerate(layer(b, z, before, now, after)):
                depth[k] = depth[k] + d
                still = jnp.exp2(depth[k])
                lit = (left[k] - still) * light
                left[k] = still
                sums[k] = [sums[k][0] + lit] + [
                    sums[k][1 + c] + lit * tints[c] for c in range(3)
                ]
            before, now = now, after
        for k in range(2):
            for c in range(4):
                inner[k, c, rows8(b), :] = sums[k][c]
            inner[k, 4, rows8(b), :] = depth[k]

    def boundary(b, slot, dst):
        def halo(side, f):
            return [
                zh[side, f, rows8(slot), pl.ds(pl.multiple_of(half * LANES, LANES), LANES)]
                for half in (hc, hh)
            ]

        front = layer(
            b, 0, [halo(0, f) for f in range(2)],
            [planes(b, f, 0) for f in range(2)], [planes(b, f, 1) for f in range(2)],
        )
        back = layer(
            b, nz - 1, [planes(b, f, nz - 2) for f in range(2)],
            [planes(b, f, nz - 1) for f in range(2)], [halo(1, f) for f in range(2)],
        )
        for k, half in enumerate((hc, hh)):
            to = pl.ds(pl.multiple_of(half * LANES, LANES), LANES)
            sums = [inner[k, c, rows8(slot), :] for c in range(4)]
            depth = inner[k, 4, rows8(slot), :]
            d0, light0, tints0 = front[k]
            d1, light1, tints1 = back[k]
            t0, t1 = jnp.exp2(d0), jnp.exp2(d0 + depth)
            whole = d0 + depth + d1
            lit0 = (1.0 - t0) * light0
            lit1 = (t1 - jnp.exp2(whole)) * light1
            base = lit0 + t0 * sums[0] + lit1
            for c in range(3):
                tone = lit0 * tints0[c] + t0 * sums[1 + c] + lit1 * tints1[c]
                dst[c, :, to] = 1.12 * (base + tone)
            dst[3, :, to] = whole

    def send(b):
        @pl.when(b != g)
        def _():
            a_copy(b, g).start()

    q0, _ = first_group(g)

    def z_wait(j, b):
        enters = jnp.where(sgn > 0, lax.rem(b, group) == 0, lax.rem(b, group) == group - 1)
        fresh = (j == 0) | (enters & (lax.div(b, group) != q0))

        @pl.when((j >= 0) & fresh)
        def _():
            for side in range(2):
                z_copy(side, lax.div(b, group), False).wait()

    def prologue(j, _):
        wait_load(j + 1)
        b = order(j)

        @pl.when(j == 0)
        def _():
            lax.fori_loop(0, ng, z_start, 0)
            y_start()

        pack(b)
        x_copy(b).start()
        return 0

    wait_load(0)
    lax.fori_loop(0, lead, prologue, 0)

    def step(i, _):
        b, ahead, behind = order(i), order(i + lead), order(i - lag)
        real = i >= lag

        @pl.when(i + lead < nb)
        def _():
            @pl.when(i + lead + 1 < nb)
            def _():
                wait_load(i + lead + 1)

        for side, at in ((0, 0), (1, nb - 1)):
            @pl.when(b == at)
            def _():
                for half in range(2):
                    y_copy(side, half, False).wait()

        x_copy(b).wait_recv()
        z_wait(i - lag, behind)

        @pl.when(i + lead < nb)
        def _():
            pack(ahead)
            x_copy(ahead).start()

        interior(b)

        @pl.when(real)
        def _():
            boundary(behind, behind, part.at[behind])
            send(behind)

        return 0

    lax.fori_loop(0, nb, step, 0)

    def tail(i, _):
        behind = order(i)
        z_wait(i, behind)
        boundary(behind, behind, part.at[behind])
        send(behind)
        return 0

    lax.fori_loop(nb - lag, nb, tail, 0)
    recv[g] = part[g]

    def arrive(j, _):
        k = wrap(g + j, nb)
        a_copy(k, k).wait_recv()
        return 0

    lax.fori_loop(1, nb, arrive, 0)
    ahead = jnp.zeros(recv.shape[2:], F32)
    sums = [jnp.zeros(recv.shape[2:], F32) for _ in range(3)]
    for k in range(nb):
        clear = jnp.exp2(ahead)
        sums = [sums[c] + clear * recv[k, c] for c in range(3)]
        ahead = ahead + recv[k, 3]
    for c in range(3):
        o_ref[c] = sums[c]
    o_ref[3] = 1.0 - jnp.exp2(ahead)

    def sent(j, _):
        a_copy(wrap(g + j, nb), g).wait_send()
        return 0

    lax.fori_loop(1, nb, sent, 0)

    def columns_sent(b, _):
        x_copy(b).wait_send()
        return 0

    lax.fori_loop(0, nb, columns_sent, 0)

    def layers_sent(q, _):
        @pl.when(g < nb - 1)
        def _():
            z_copy(0, q, True).wait_send()

        @pl.when(g > 0)
        def _():
            z_copy(1, q, True).wait_send()

        return 0

    lax.fori_loop(0, ng, layers_sent, 0)
    for half in range(2):
        @pl.when(iy < n_iy - 1)
        def _():
            y_copy(0, half, True).wait_send()

        @pl.when(iy > 0)
        def _():
            y_copy(1, half, True).wait_send()


def body(sizes, fields, palette):
    n_gz = sizes[2]
    _, nz, ny, nx = fields.shape
    group = 4 if n_gz % 4 == 0 and n_gz > 4 else 1
    lag, lead = (4, 2) if n_gz > 4 else (2, 1)
    dma = pltpu.SemaphoreType.DMA
    return pl.pallas_call(
        functools.partial(kernel, sizes, lag, lead, group),
        out_shape=jax.ShapeDtypeStruct((4, ny // n_gz, nx), F32),
        in_specs=[
            pl.BlockSpec(memory_space=pltpu.SMEM),
            pl.BlockSpec(memory_space=pl.ANY),
        ],
        out_specs=pl.BlockSpec(memory_space=pltpu.VMEM),
        scratch_shapes=[
            pltpu.VMEM((2, 2, nz, ny + 2 * ROWS, LANES), F32),
            pltpu.VMEM((2, 2, ny, nx), F32),
            pltpu.VMEM((2, ny, LANES), F32),
            pltpu.VMEM((2, ny, LANES), F32),
            pltpu.VMEM((2, 5, ny, LANES), F32),
            pltpu.VMEM((n_gz, 4, ROWS, nx), F32),
            pltpu.VMEM((n_gz, 4, ROWS, nx), F32),
            dma((n_gz, 2)),
            dma((2, n_gz // group)),
            dma((2, n_gz // group)),
            dma((2, 2)),
            dma((2, 2)),
            dma((n_gz,)),
            dma((n_gz,)),
            dma((n_gz,)),
            dma((n_gz,)),
        ],
        compiler_params=pltpu.CompilerParams(
            collective_id=0, has_side_effects=True, vmem_limit_bytes=40 << 20
        ),
    )(palette, fields)


def solution(mesh):
    sizes = tuple(mesh.shape[axis] for axis in ("iy", "ix", "gz"))
    return jax.shard_map(
        functools.partial(body, sizes),
        mesh=mesh,
        in_specs=(P(None, "gz", "iy", "ix"), P()),
        out_specs=P(None, ("iy", "gz"), "ix"),
        check_vma=False,
    )
```

```python
import functools

import jax
import jax.numpy as jnp
from jax import lax
from jax.experimental import pallas as pl
from jax.experimental.pallas import tpu as pltpu
from jax.sharding import PartitionSpec as P

MESH = pl.DeviceIdType.MESH
F32 = jnp.float32
LANES = 128
ROWS = 8
LOG2E = 1.4426950408889634
C1 = 0.005 * LOG2E
C2 = 0.016 * LOG2E


def cell(dz, dy, dx, s, ez, ey, ex, u, pal, nz, ny):
    r = lax.rsqrt(dz * dz + dy * dy + dx * dx + 4.0)
    depth = jnp.exp2(s * LOG2E) * (C2 * (r * r) - C1)
    face = jnp.abs(nz * dz + ny * dy + dx) * r + 0.3 / 0.56
    around = pltpu.reciprocal(ez * ez + ey * ey + ex * ex + 4.0, approx=True)
    light = face * (0.375 - around)
    tints = [jnp.tanh(pal[0][c] * u + pal[1][c]) for c in range(3)]
    return depth, light, tints


def kernel(
    sizes, early, lead, group,
    p_ref, f_ref, o_ref,
    pal_ref, vol, zh, hs, hx, inner, part, recv,
    pal_sem, load_sem, zsend, zrecv, ysend, yrecv, xsend, xrecv, asend, arecv,
):
    n_iy, n_ix, n_gz = sizes
    nz, ny = f_ref.shape[1], f_ref.shape[2]
    nb = n_gz
    ng = nb // group
    iy, ix, g = lax.axis_index("iy"), lax.axis_index("ix"), lax.axis_index("gz")
    sgn = jnp.where(g < nb // 2, 1, -1)
    hh, hc = 1 - ix, ix
    top, bottom = ROWS - 1, ROWS + ny

    def wrap(i, n):
        return lax.rem(i + 2 * n, n)

    def order(i):
        return wrap(g + sgn * (i + 1), nb)

    def rows8(b):
        return pl.ds(pl.multiple_of(ROWS * b, ROWS), ROWS)

    def shifted(b, by):
        return pl.ds(pl.multiple_of(ROWS * b, ROWS) + by, ROWS)

    def load(l, half):
        b = wrap(g + sgn * l, nb)
        return pltpu.make_async_copy(
            f_ref.at[:, :, rows8(b), pl.ds(half * LANES, LANES)],
            vol.at[half, :, :, shifted(b, ROWS), :],
            load_sem.at[l, half],
        )

    def start_load(l, _):
        for half in range(2):
            load(l, half).start()
        return 0

    def wait_load(l):
        for half in range(2):
            load(l, half).wait()

    colors = pltpu.make_async_copy(p_ref, pal_ref, pal_sem)
    colors.start()
    lax.fori_loop(0, lead + 2, start_load, 0)

    barrier = pltpu.get_barrier_semaphore()

    def greet(j, _):
        pl.semaphore_signal(
            barrier, inc=1, device_id={"gz": wrap(g + j, nb)}, device_id_type=MESH
        )
        return 0

    lax.fori_loop(1, nb, greet, 0)
    pl.semaphore_signal(barrier, inc=1, device_id={"ix": 1 - ix}, device_id_type=MESH)

    @pl.when(iy > 0)
    def _():
        pl.semaphore_signal(barrier, inc=1, device_id={"iy": iy - 1}, device_id_type=MESH)

    @pl.when(iy < n_iy - 1)
    def _():
        pl.semaphore_signal(barrier, inc=1, device_id={"iy": iy + 1}, device_id_type=MESH)

    lax.fori_loop(lead + 2, nb, start_load, 0)

    def y_copy(side, half, remote):
        source = 0 if remote == (side == 1) else ny - 1
        src = f_ref.at[:, :, pl.ds(source, 1), pl.ds(half * LANES, LANES)]
        dst = vol.at[half, :, :, pl.ds(bottom if side else top, 1), :]
        if not remote:
            return pltpu.make_async_copy(src, dst, yrecv.at[side, half])
        return pltpu.make_async_remote_copy(
            src, dst, ysend.at[side, half], yrecv.at[side, half],
            device_id={"iy": iy - 1 if side else iy + 1}, device_id_type=MESH,
        )

    def z_rows(q):
        n = ROWS * group
        return pl.ds(pl.multiple_of(q * n, n), n)

    def z_copy(side, q, remote):
        source = 0 if remote == (side == 1) else nz - 1
        src = f_ref.at[:, source, z_rows(q), :]
        dst = zh.at[side, :, z_rows(q), :]
        if not remote:
            return pltpu.make_async_copy(src, dst, zrecv.at[side, q])
        return pltpu.make_async_remote_copy(
            src, dst, zsend.at[side, q], zrecv.at[side, q],
            device_id={"gz": g - 1 if side else g + 1}, device_id_type=MESH,
        )

    def first_group(gg):
        sg = jnp.where(gg < nb // 2, 1, -1)
        return lax.div(wrap(gg + sg, nb), group), sg

    def z_start(j, _):
        @pl.when(g < nb - 1)
        def _():
            q0, sg = first_group(g + 1)
            z_copy(0, wrap(q0 + sg * j, ng), True).start()

        @pl.when(g > 0)
        def _():
            q0, sg = first_group(g - 1)
            z_copy(1, wrap(q0 + sg * j, ng), True).start()

        @pl.when(g == 0)
        def _():
            z_copy(0, j, False).start()

        @pl.when(g == nb - 1)
        def _():
            z_copy(1, j, False).start()

        return 0

    def y_start():
        for half in range(2):
            @pl.when(iy < n_iy - 1)
            def _():
                y_copy(0, half, True).start()

            @pl.when(iy > 0)
            def _():
                y_copy(1, half, True).start()

            @pl.when(iy == 0)
            def _():
                y_copy(0, half, False).start()

            @pl.when(iy == n_iy - 1)
            def _():
                y_copy(1, half, False).start()

    lane = lax.broadcasted_iota(jnp.int32, (ROWS, LANES), 1)
    out_roll = jnp.where(ix == 0, LANES - 1, 1)
    in_roll = LANES - out_roll
    edge = jnp.where(ix == 0, LANES - 1, 0)
    at_edge = lane == edge
    at_inner = lane == LANES - 1 - edge
    nz_dir = jnp.where(ix == 0, 0.45, -0.45).astype(F32)
    ny_dir = jnp.where(ix == 0, 0.6, -0.6).astype(F32)
    colors.wait()
    pal = [[0.5 * pal_ref[i, c] for c in range(3)] for i in range(2)]

    def pack(b, slot):
        for f in range(2):
            acc = None
            for z in range(nz):
                column = pltpu.roll(
                    vol[hh, f, z, shifted(b, ROWS), :], lax.rem(z - edge + LANES, LANES), 1
                )
                acc = column if acc is None else jnp.where(lane == z, column, acc)
            hs[f, rows8(slot), :] = acc

    def x_copy(b):
        return pltpu.make_async_remote_copy(
            hs.at[:, rows8(b), :], hx.at[:, rows8(b), :], xsend.at[b], xrecv.at[b],
            device_id={"ix": 1 - ix}, device_id_type=MESH,
        )

    def a_copy(b, slot):
        return pltpu.make_async_remote_copy(
            part.at[b], recv.at[slot], asend.at[b], arecv.at[slot],
            device_id={"gz": b}, device_id_type=MESH,
        )

    def planes(b, f, z):
        return [vol[half, f, z, shifted(b, ROWS), :] for half in (hc, hh)]

    def layer(b, z, before, now, after):
        diffs = []
        for f in range(2):
            c, h = now[f]
            beside = pltpu.roll(hx[f, rows8(b), :], lax.rem(edge - z + LANES, LANES), 1)
            oc, oh = pltpu.roll(c, out_roll, 1), pltpu.roll(h, out_roll, 1)
            ic, ih = pltpu.roll(c, in_roll, 1), pltpu.roll(h, in_roll, 1)
            dx = [
                jnp.where(at_edge, oh, oc) - jnp.where(at_inner, c, ic),
                jnp.where(at_edge, beside, oh) - jnp.where(at_inner, ic, ih),
            ]
            dy = [
                vol[half, f, z, shifted(b, ROWS + 1), :] - vol[half, f, z, shifted(b, ROWS - 1), :]
                for half in (hc, hh)
            ]
            dz = [after[f][k] - before[f][k] for k in range(2)]
            diffs.append((dz, dy, dx))
        (dz, dy, dx), (ez, ey, ex) = diffs
        return [
            cell(
                dz[k], dy[k], dx[k], now[0][k], ez[k], ey[k], ex[k], now[1][k],
                pal, nz_dir, ny_dir,
            )
            for k in range(2)
        ]

    def halo(b, side, f):
        return [
            zh[side, f, rows8(b), pl.ds(pl.multiple_of(half * LANES, LANES), LANES)]
            for half in (hc, hh)
        ]

    def render(b, first, last):
        zero, one = jnp.zeros((ROWS, LANES), F32), jnp.ones((ROWS, LANES), F32)
        depth, left = [zero, zero], [one, one]
        sums = [[zero] * 4, [zero] * 4]

        def plane(z):
            if z < 0 or z >= nz:
                return [halo(b, 0 if z < 0 else 1, f) for f in range(2)]
            return [planes(b, f, z) for f in range(2)]

        before, now = plane(first - 1), plane(first)
        for z in range(first, last + 1):
            after = plane(z + 1)
            for k, (d, light, tints) in enumerate(layer(b, z, before, now, after)):
                depth[k] = depth[k] + d
                still = jnp.exp2(depth[k])
                lit = (left[k] - still) * light
                left[k] = still
                sums[k] = [sums[k][0] + lit] + [
                    sums[k][1 + c] + lit * tints[c] for c in range(3)
                ]
            before, now = now, after
        return sums, depth

    def interior(b, i):
        sums, depth = render(b, 1, nz - 2)
        for k in range(2):
            for c in range(4):
                inner[i, k, c] = sums[k][c]
            inner[i, k, 4] = depth[k]

    def boundary(b, i):
        front = layer(
            b, 0, [halo(b, 0, f) for f in range(2)],
            [planes(b, f, 0) for f in range(2)], [planes(b, f, 1) for f in range(2)],
        )
        back = layer(
            b, nz - 1, [planes(b, f, nz - 2) for f in range(2)],
            [planes(b, f, nz - 1) for f in range(2)], [halo(b, 1, f) for f in range(2)],
        )
        for k, half in enumerate((hc, hh)):
            sums = [inner[i, k, c] for c in range(4)]
            depth = inner[i, k, 4]
            d0, light0, tints0 = front[k]
            d1, light1, tints1 = back[k]
            t0, t1 = jnp.exp2(d0), jnp.exp2(d0 + depth)
            whole = d0 + depth + d1
            lit0 = (1.0 - t0) * light0
            lit1 = (t1 - jnp.exp2(whole)) * light1
            keep(
                b, half,
                [lit0 + t0 * sums[0] + lit1]
                + [lit0 * tints0[c] + t0 * sums[1 + c] + lit1 * tints1[c] for c in range(3)],
                whole,
            )

    def keep(b, half, sums, depth):
        to = pl.ds(pl.multiple_of(half * LANES, LANES), LANES)
        for c in range(3):
            part[b, c, :, to] = 1.12 * (sums[0] + sums[1 + c])
        part[b, 3, :, to] = depth

    def send(b):
        @pl.when(b != g)
        def _():
            a_copy(b, g).start()

    q0, _ = first_group(g)

    def z_wait(j, b):
        enters = jnp.where(sgn > 0, lax.rem(b, group) == 0, lax.rem(b, group) == group - 1)
        fresh = (j == 0) | (enters & (lax.div(b, group) != q0))

        @pl.when((j >= 0) & fresh)
        def _():
            for side in range(2):
                z_copy(side, lax.div(b, group), False).wait()

    for l in range(lead + 1):
        wait_load(l)
    for j in range(lead):
        pack(order(j), order(j))
    pl.semaphore_wait(barrier, nb + jnp.where(iy > 0, 1, 0) + jnp.where(iy < n_iy - 1, 1, 0))
    for j in range(lead):
        x_copy(order(j)).start()
    lax.fori_loop(0, ng, z_start, 0)
    y_start()

    def wait_step(i):
        b = order(i)

        @pl.when(i + lead + 1 < nb)
        def _():
            wait_load(i + lead + 1)

        for side, at in ((0, 0), (1, nb - 1)):
            @pl.when(b == at)
            def _():
                for half in range(2):
                    y_copy(side, half, False).wait()

        x_copy(b).wait_recv()
        return b

    def pack_ahead(i):
        ahead = order(jnp.minimum(i + lead, nb - 1))
        pack(ahead, jnp.where(i + lead < nb, ahead, nb))

    def send_ahead(i):
        @pl.when(i + lead < nb)
        def _():
            x_copy(order(i + lead)).start()

    def early_step(i, _):
        b = wait_step(i)
        pack_ahead(i)
        interior(b, i)
        send_ahead(i)
        return 0

    lax.fori_loop(0, early, early_step, 0)
    for i in range(early):
        z_wait(i, order(i))
    for i in range(early):
        boundary(order(i), i)
    for i in range(early):
        send(order(i))

    def late_step(i, _):
        b = wait_step(i)
        z_wait(i, b)
        pack_ahead(i)
        sums, depth = render(b, 0, nz - 1)
        for k, half in enumerate((hc, hh)):
            keep(b, half, sums[k], depth[k])
        send_ahead(i)
        send(b)
        return 0

    lax.fori_loop(early, nb, late_step, 0)
    recv[g] = part[g]

    def sent(j, _):
        a_copy(wrap(g + j, nb), g).wait_send()
        return 0

    lax.fori_loop(1, nb, sent, 0)

    def columns_sent(b, _):
        x_copy(b).wait_send()
        return 0

    lax.fori_loop(0, nb, columns_sent, 0)

    def layers_sent(q, _):
        @pl.when(g < nb - 1)
        def _():
            z_copy(0, q, True).wait_send()

        @pl.when(g > 0)
        def _():
            z_copy(1, q, True).wait_send()

        return 0

    lax.fori_loop(0, ng, layers_sent, 0)
    for half in range(2):
        @pl.when(iy < n_iy - 1)
        def _():
            y_copy(0, half, True).wait_send()

        @pl.when(iy > 0)
        def _():
            y_copy(1, half, True).wait_send()

    def arrive(j, _):
        k = wrap(g + j, nb)
        a_copy(k, k).wait_recv()
        return 0

    lax.fori_loop(1, nb, arrive, 0)
    ahead = jnp.zeros(recv.shape[2:], F32)
    sums = [jnp.zeros(recv.shape[2:], F32) for _ in range(3)]
    for k in range(nb):
        clear = jnp.exp2(ahead)
        sums = [sums[c] + clear * recv[k, c] for c in range(3)]
        ahead = ahead + recv[k, 3]
    for c in range(3):
        o_ref[c] = sums[c]
    o_ref[3] = 1.0 - jnp.exp2(ahead)


def body(sizes, fields, palette):
    n_gz = sizes[2]
    _, nz, ny, nx = fields.shape
    group = 4 if n_gz % 4 == 0 and n_gz > 4 else 1
    early, lead = (6, 4) if n_gz > 4 else (2, 1)
    dma = pltpu.SemaphoreType.DMA
    return pl.pallas_call(
        functools.partial(kernel, sizes, early, lead, group),
        out_shape=jax.ShapeDtypeStruct((4, ny // n_gz, nx), F32),
        in_specs=[
            pl.BlockSpec(memory_space=pl.ANY),
            pl.BlockSpec(memory_space=pl.ANY),
        ],
        out_specs=pl.BlockSpec(memory_space=pltpu.VMEM),
        scratch_shapes=[
            pltpu.SMEM((2, 3), F32),
            pltpu.VMEM((2, 2, nz, ny + 2 * ROWS, LANES), F32),
            pltpu.VMEM((2, 2, ny, nx), F32),
            pltpu.VMEM((2, ny + ROWS, LANES), F32),
            pltpu.VMEM((2, ny, LANES), F32),
            pltpu.VMEM((early, 2, 5, ROWS, LANES), F32),
            pltpu.VMEM((n_gz, 4, ROWS, nx), F32),
            pltpu.VMEM((n_gz, 4, ROWS, nx), F32),
            dma(()),
            dma((n_gz, 2)),
            dma((2, n_gz // group)),
            dma((2, n_gz // group)),
            dma((2, 2)),
            dma((2, 2)),
            dma((n_gz,)),
            dma((n_gz,)),
            dma((n_gz,)),
            dma((n_gz,)),
        ],
        compiler_params=pltpu.CompilerParams(
            collective_id=0, has_side_effects=True, vmem_limit_bytes=60 << 20
        ),
    )(palette, fields)


def solution(mesh):
    sizes = tuple(mesh.shape[axis] for axis in ("iy", "ix", "gz"))
    return jax.shard_map(
        functools.partial(body, sizes),
        mesh=mesh,
        in_specs=(P(None, "gz", "iy", "ix"), P()),
        out_specs=P(None, ("iy", "gz"), "ix"),
        check_vma=False,
    )
```

```python
import functools

import jax
import jax.numpy as jnp
from jax import lax
from jax.experimental import pallas as pl
from jax.experimental.pallas import tpu as pltpu
from jax.sharding import PartitionSpec as P

MESH = pl.DeviceIdType.MESH
F32 = jnp.float32
LANES = 128
ROWS = 8
LOG2E = 1.4426950408889634
C1 = 0.005 * LOG2E
C2 = 0.016 * LOG2E


def cell(dz, dy, dx, s, ez, ey, ex, u, pal, nz, ny):
    r = lax.rsqrt(dz * dz + dy * dy + dx * dx + 4.0)
    depth = jnp.exp2(s * LOG2E) * (C2 * (r * r) - C1)
    face = jnp.abs(nz * dz + ny * dy + dx) * r + 0.3 / 0.56
    around = pltpu.reciprocal(ez * ez + ey * ey + ex * ex + 4.0, approx=True)
    light = face * (0.375 - around)
    tints = [jnp.tanh(pal[0][c] * u + pal[1][c]) for c in range(3)]
    return depth, light, tints


def kernel(
    sizes, gap, entry, pair,
    p_ref, f_ref, o_ref,
    pal_ref, vol, zh, hs, hx, outs, ins, inner, part, recv,
    pal_sem, all_sem, load_sem, zsend, zrecv, ysend, yrecv, xsend, xrecv, asend, arecv,
):
    n_iy, n_ix, n_gz = sizes
    nz, ny = f_ref.shape[1], f_ref.shape[2]
    nb = n_gz
    iy, ix, g = lax.axis_index("iy"), lax.axis_index("ix"), lax.axis_index("gz")
    sgn = jnp.where(g < nb // 2, 1, -1)
    hh, hc = 1 - ix, ix
    top, bottom = ROWS - 1, ROWS + ny

    def wrap(i, n):
        return lax.rem(i + 2 * n, n)

    def order(i):
        return wrap(g + sgn * (i + 1), nb)

    ring = 4 if nb > 4 else nb
    cols = nb // ring
    gx, gy = lax.div(g, ring), lax.rem(g, ring)

    def hops(o):
        dx, dy = o // ring, o % ring
        return min(dx, cols - dx) + min(dy, ring - dy)

    turns = sorted(range(nb), key=lambda o: (-hops(o), -min(o % ring, ring - o % ring), o))

    def far_first(j, gx, gy):
        o = jnp.int32(0)
        for k, turn in enumerate(turns):
            o = o + jnp.where(j == k, turn, 0)
        return wrap(gx + lax.div(o, ring), cols) * ring + wrap(gy + lax.rem(o, ring), ring)

    def rows8(b):
        return pl.ds(pl.multiple_of(ROWS * b, ROWS), ROWS)

    def shifted(b, by):
        return pl.ds(pl.multiple_of(ROWS * b, ROWS) + by, ROWS)

    def load(l, half):
        b = wrap(g + sgn * l, nb)
        return pltpu.make_async_copy(
            f_ref.at[:, :, rows8(b), pl.ds(half * LANES, LANES)],
            vol.at[half, :, :, shifted(b, ROWS), :],
            load_sem.at[l],
        )

    def start_load(l, _):
        for half in range(2):
            load(l, half).start()
        return 0

    def landed(ref, sem):
        pltpu.make_async_copy(ref, ref, sem).wait()

    def wait_load(l):
        landed(vol.at[:, :, :, pl.ds(ROWS, ROWS), :], load_sem.at[l])

    colors = pltpu.make_async_copy(p_ref, pal_ref, pal_sem)
    colors.start()
    lax.fori_loop(0, pair + 2, start_load, 0)

    barrier = pltpu.get_barrier_semaphore()

    def to_row(j):
        return {"gz": gx * ring + wrap(gy + j, ring)}

    def to_col(j):
        return {"gz": wrap(gx + j, cols) * ring + gy}

    def hello(sem, where):
        pl.semaphore_signal(sem, inc=1, device_id=where, device_id_type=MESH)

    skew_up = (gy == ring - 1) & (g < nb - 1)
    skew_down = (gy == 0) & (g > 0)

    hello(barrier, {"ix": 1 - ix})
    for there, where in (
        (iy > 0, {"iy": iy - 1}),
        (iy < n_iy - 1, {"iy": iy + 1}),
        (skew_up, {"gz": g + 1}),
        (skew_down, {"gz": g - 1}),
    ):
        @pl.when(there)
        def _(where=where):
            hello(barrier, where)
    for j in range(1, ring):
        hello(barrier, to_row(j))
    for j in range(1, cols):
        hello(barrier, to_col(j))
    beside = 1 + (ring - 1) + (cols - 1)
    for there in (iy > 0, iy < n_iy - 1, skew_up, skew_down):
        beside = beside + jnp.where(there, 1, 0)

    lax.fori_loop(pair + 2, nb, start_load, 0)

    def y_copy(side, half, remote):
        source = 0 if remote == (side == 1) else ny - 1
        src = f_ref.at[:, :, pl.ds(source, 1), pl.ds(half * LANES, LANES)]
        dst = vol.at[half, :, :, pl.ds(bottom if side else top, 1), :]
        if not remote:
            return pltpu.make_async_copy(src, dst, yrecv.at[side])
        return pltpu.make_async_remote_copy(
            src, dst, ysend.at[side], yrecv.at[side],
            device_id={"iy": iy - 1 if side else iy + 1}, device_id_type=MESH,
        )

    def z_copy(side, b, remote):
        source = 0 if remote == (side == 1) else nz - 1
        src = f_ref.at[:, source, rows8(b), :]
        dst = zh.at[side, :, rows8(b), :]
        if not remote:
            return pltpu.make_async_copy(src, dst, zrecv.at[b])
        return pltpu.make_async_remote_copy(
            src, dst, zsend.at[side], zrecv.at[b],
            device_id={"gz": g - 1 if side else g + 1}, device_id_type=MESH,
        )

    def z_start(j, _):
        @pl.when(g < nb - 1)
        def _():
            z_copy(0, far_first(j, lax.div(g + 1, ring), lax.rem(g + 1, ring)), True).start()

        @pl.when(g > 0)
        def _():
            z_copy(1, far_first(j, lax.div(g - 1, ring), lax.rem(g - 1, ring)), True).start()

        @pl.when(g == 0)
        def _():
            z_copy(0, j, False).start()

        @pl.when(g == nb - 1)
        def _():
            z_copy(1, j, False).start()

        return 0

    def y_start():
        for half in range(2):
            @pl.when(iy < n_iy - 1)
            def _():
                y_copy(0, half, True).start()

            @pl.when(iy > 0)
            def _():
                y_copy(1, half, True).start()

            @pl.when(iy == 0)
            def _():
                y_copy(0, half, False).start()

            @pl.when(iy == n_iy - 1)
            def _():
                y_copy(1, half, False).start()

    lane = lax.broadcasted_iota(jnp.int32, (ROWS, LANES), 1)
    out_roll = jnp.where(ix == 0, LANES - 1, 1)
    in_roll = LANES - out_roll
    edge = jnp.where(ix == 0, LANES - 1, 0)
    at_edge = lane == edge
    at_inner = lane == LANES - 1 - edge
    nz_dir = jnp.where(ix == 0, 0.45, -0.45).astype(F32)
    ny_dir = jnp.where(ix == 0, 0.6, -0.6).astype(F32)
    colors.wait()
    pal = [[0.5 * pal_ref[i, c] for c in range(3)] for i in range(2)]

    def spread(z, side):
        return 2 * z + 1 if z % 2 == 0 else 2 * z - 1 + side

    def pack(b, f, edges):
        side = jnp.where(ix == 0, -1, 1)
        acc = None
        for z in range(0, nz, 2):
            both = jnp.where(at_edge, edges[z][0], edges[z + 1][1])
            to = spread(z, side)
            both = pltpu.roll(both, lax.rem(to - edge + LANES, LANES), 1)
            acc = both if acc is None else jnp.where(lane >= to - 1, both, acc)
        hs[f, rows8(b), :] = acc

    def x_copy(b):
        return pltpu.make_async_remote_copy(
            hs.at[:, rows8(b), :], hx.at[:, rows8(b), :], xsend, xrecv.at[b],
            device_id={"ix": 1 - ix}, device_id_type=MESH,
        )

    def a_copy(b, slot):
        return pltpu.make_async_remote_copy(
            part.at[b], recv.at[slot], asend, arecv,
            device_id={"gz": b}, device_id_type=MESH,
        )

    def planes(b, f, z):
        return [vol[half, f, z, shifted(b, ROWS), :] for half in (hc, hh)]

    def at(half, f, z, b):
        return vol[half, f, z, shifted(b, ROWS), :]

    def dy_of(half, f, z, b):
        return vol[half, f, z, shifted(b, ROWS + 1), :] - vol[half, f, z, shifted(b, ROWS - 1), :]

    def beyond(side, f, half, b):
        return zh[side, f, rows8(b), pl.ds(pl.multiple_of(half * LANES, LANES), LANES)]

    def column(half, f, z, b):
        if z < 0:
            return beyond(0, f, half, b)
        if z >= nz:
            return beyond(1, f, half, b)
        return at(half, f, z, b)

    def dz_of(half, f, z, b):
        return column(half, f, z + 1, b) - column(half, f, z - 1, b)

    def inner_dx(f, z, b, now, out):
        inward = pltpu.roll(now, in_roll, 1)
        dx = jnp.where(at_edge, out, pltpu.roll(now, out_roll, 1)) - jnp.where(at_inner, now, inward)
        return dx, inward

    def outer_dx(f, z, b, now, out, inward):
        side = jnp.where(ix == 0, 1, -1)
        beside = pltpu.roll(hx[f, rows8(b), :], lax.rem(edge - spread(z, side) + LANES, LANES), 1)
        return jnp.where(at_edge, beside, out) - jnp.where(at_inner, inward, pltpu.roll(now, in_roll, 1))

    def shade(half, z, b, now, dx):
        dz = [dz_of(half, f, z, b) for f in range(2)]
        dy = [dy_of(half, f, z, b) for f in range(2)]
        return cell(
            dz[0], dy[0], dx[0], now[0], dz[1], dy[1], dx[1], now[1], pal, nz_dir, ny_dir
        )

    def clean():
        zero, one = jnp.zeros((ROWS, LANES), F32), jnp.ones((ROWS, LANES), F32)
        return [zero, one] + [zero] * 4

    def add(state, d, light, tints):
        depth = state[0] + d
        still = jnp.exp2(depth)
        lit = (state[1] - still) * light
        return [depth, still, state[2] + lit] + [state[3 + c] + lit * tints[c] for c in range(3)]

    def inner_half(blocks):
        states = [clean() for _ in blocks]
        edges = [[[] for _ in range(2)] for _ in blocks]
        for z in range(nz):
            for k, b in enumerate(blocks):
                now, dx = [], []
                for f in range(2):
                    h = at(hh, f, z, b)
                    out = pltpu.roll(h, out_roll, 1)
                    outs[f, z, rows8(b), :] = out
                    edges[k][f].append((h, out))
                    if 0 < z < nz - 1:
                        now.append(at(hc, f, z, b))
                        d, inward = inner_dx(f, z, b, now[f], out)
                        ins[f, z, rows8(b), :] = inward
                        dx.append(d)
                if 0 < z < nz - 1:
                    states[k] = add(states[k], *shade(hc, z, b, now, dx))
        for k, b in enumerate(blocks):
            for f in range(2):
                pack(b, f, edges[k][f])
            for c in range(6):
                inner[b, c] = states[k][c]

    def outer_half(blocks):
        ends = [{} for _ in blocks]
        states = [clean() for _ in blocks]
        for z in range(nz):
            for k, b in enumerate(blocks):
                now = [at(hh, f, z, b) for f in range(2)]
                out = [outs[f, z, rows8(b), :] for f in range(2)]
                if 0 < z < nz - 1:
                    inward = [ins[f, z, rows8(b), :] for f in range(2)]
                else:
                    mine = [at(hc, f, z, b) for f in range(2)]
                    pairs = [inner_dx(f, z, b, mine[f], out[f]) for f in range(2)]
                    inward = [p[1] for p in pairs]
                    ends[k][z] = shade(hc, z, b, mine, [p[0] for p in pairs])
                dx = [outer_dx(f, z, b, now[f], out[f], inward[f]) for f in range(2)]
                states[k] = add(states[k], *shade(hh, z, b, now, dx))
        for k, b in enumerate(blocks):
            keep(b, hh, states[k])
            (d0, light0, tints0), (d1, light1, tints1) = ends[k][0], ends[k][nz - 1]
            mid = [inner[b, c] for c in range(6)]
            t0 = jnp.exp2(d0)
            lit0 = (1.0 - t0) * light0
            depth = d0 + mid[0] + d1
            lit1 = (t0 * mid[1] - jnp.exp2(depth)) * light1
            sums = [lit0 + t0 * mid[2] + lit1] + [
                lit0 * tints0[c] + t0 * mid[3 + c] + lit1 * tints1[c] for c in range(3)
            ]
            keep(b, hc, [depth, None] + sums)

    def keep(b, half, state):
        to = pl.ds(pl.multiple_of(half * LANES, LANES), LANES)
        for c in range(3):
            part[b, c, :, to] = 1.12 * (state[2] + state[3 + c])
        part[b, 3, :, to] = state[0]

    def send(b):
        @pl.when(b != g)
        def _():
            a_copy(b, g).start()

    for l in range(2):
        wait_load(l)

    def enter():
        pl.semaphore_wait(barrier, beside)
        for j in range(1, cols):
            hello(all_sem, to_col(j))
        y_start()

        def columns(i, _):
            x_copy(order(i)).start()
            return 0

        lax.fori_loop(0, entry, columns, 0)
        lax.fori_loop(0, nb, z_start, 0)

    def step(s, _):
        @pl.when(s == entry // pair)
        def _():
            enter()

        i = s * pair

        @pl.when(i < nb)
        def _():
            for k in range(pair):
                @pl.when(i + k + 2 < nb)
                def _():
                    wait_load(i + k + 2)

                for side, row in ((0, 0), (1, nb - 1)):
                    @pl.when(order(i + k) == row)
                    def _():
                        landed(vol.at[:, :, :, pl.ds(0, 1), :], yrecv.at[side])

            inner_half([order(i + k) for k in range(pair)])

            @pl.when(i >= entry)
            def _():
                for k in range(pair):
                    x_copy(order(i + k)).start()

        @pl.when(i == gap)
        def _():
            if cols > 1:
                pl.semaphore_wait(all_sem, cols - 1)

        @pl.when(i >= gap)
        def _():
            j = i - gap
            blocks = [far_first(j + k, gx, gy) for k in range(pair)]
            for k in range(pair):
                x_copy(blocks[k]).wait_recv()
                landed(zh.at[:, :, rows8(blocks[k]), :], zrecv.at[blocks[k]])
            outer_half(blocks)
            for k in range(pair):
                send(blocks[k])

        return 0

    lax.fori_loop(0, (nb + gap) // pair, step, 0)
    recv[g] = part[g]
    landed(hs, xsend)

    @pl.when(g < nb - 1)
    def _():
        landed(zh.at[0], zsend.at[0])

    @pl.when(g > 0)
    def _():
        landed(zh.at[1], zsend.at[1])

    for side, there in ((0, iy < n_iy - 1), (1, iy > 0)):
        @pl.when(there)
        def _(side=side):
            landed(vol.at[:, :, :, pl.ds(0, 1), :], ysend.at[side])

    landed(part.at[pl.ds(0, nb - 1)], asend)
    landed(recv.at[pl.ds(0, nb - 1)], arecv)
    ahead = jnp.zeros(recv.shape[2:], F32)
    sums = [jnp.zeros(recv.shape[2:], F32) for _ in range(3)]
    for k in range(nb):
        clear = jnp.exp2(ahead)
        sums = [sums[c] + clear * recv[k, c] for c in range(3)]
        ahead = ahead + recv[k, 3]
    for c in range(3):
        o_ref[c] = sums[c]
    o_ref[3] = 1.0 - jnp.exp2(ahead)


def body(sizes, fields, palette):
    n_gz = sizes[2]
    _, nz, ny, nx = fields.shape
    gap, entry, pair = (16, 2, 1) if n_gz > 4 else (4, 1, 1)
    dma = pltpu.SemaphoreType.DMA
    return pl.pallas_call(
        functools.partial(kernel, sizes, gap, entry, pair),
        out_shape=jax.ShapeDtypeStruct((4, ny // n_gz, nx), F32),
        in_specs=[
            pl.BlockSpec(memory_space=pl.ANY),
            pl.BlockSpec(memory_space=pl.ANY),
        ],
        out_specs=pl.BlockSpec(memory_space=pltpu.VMEM),
        scratch_shapes=[
            pltpu.SMEM((2, 3), F32),
            pltpu.VMEM((2, 2, nz, ny + 2 * ROWS, LANES), F32),
            pltpu.VMEM((2, 2, ny, nx), F32),
            pltpu.VMEM((2, ny, LANES), F32),
            pltpu.VMEM((2, ny, LANES), F32),
            pltpu.VMEM((2, nz, ny, LANES), F32),
            pltpu.VMEM((2, nz, ny, LANES), F32),
            pltpu.VMEM((n_gz, 6, ROWS, LANES), F32),
            pltpu.VMEM((n_gz, 4, ROWS, nx), F32),
            pltpu.VMEM((n_gz, 4, ROWS, nx), F32),
            dma(()),
            pltpu.SemaphoreType.REGULAR,
            dma((n_gz,)),
            dma((2,)),
            dma((n_gz,)),
            dma((2,)),
            dma((2,)),
            dma(()),
            dma((n_gz,)),
            dma(()),
            dma(()),
        ],
        compiler_params=pltpu.CompilerParams(
            collective_id=0, has_side_effects=True, vmem_limit_bytes=58 << 20
        ),
    )(palette, fields)


def solution(mesh):
    sizes = tuple(mesh.shape[axis] for axis in ("iy", "ix", "gz"))
    return jax.shard_map(
        functools.partial(body, sizes),
        mesh=mesh,
        in_specs=(P(None, "gz", "iy", "ix"), P()),
        out_specs=P(None, ("iy", "gz"), "ix"),
        check_vma=False,
    )
```

```python
import functools

import jax
import jax.numpy as jnp
from jax import lax
from jax.experimental import pallas as pl
from jax.experimental.pallas import tpu as pltpu
from jax.sharding import PartitionSpec as P

MESH = pl.DeviceIdType.MESH

F32 = jnp.float32
LANES = 128
ROWS = 8
LOG2E = 1.4426950408889634
C1 = 0.005 * LOG2E
C2 = 0.016 * LOG2E

def cell(dz, dy, dx, s, ez, ey, ex, u, pal, nz, ny):
    r = lax.rsqrt(dz * dz + dy * dy + dx * dx + 4.0)
    depth = jnp.exp2(s * LOG2E) * (C2 * (r * r) - C1)
    face = jnp.abs(nz * dz + ny * dy + dx) * r + 0.3 / 0.56
    around = pltpu.reciprocal(ez * ez + ey * ey + ex * ex + 4.0, approx=True)
    light = face * (0.375 - around)
    tints = [jnp.tanh(pal[0][c] * u + pal[1][c]) for c in range(3)]
    return depth, light, tints

def kernel(
    sizes, gap, entry, pair, cut,
    p_ref, f_ref, o_ref,
    pal_ref, vol, zh, hs, hx, outs, ins, inner, part, recv,
    pal_sem, all_sem, load_sem, zsend, zrecv, ysend, yrecv, xsend, xrecv, asend, arecv,
):
    n_iy, n_ix, n_gz = sizes
    nz, ny = f_ref.shape[1], f_ref.shape[2]
    nb = n_gz
    iy, ix, g = lax.axis_index("iy"), lax.axis_index("ix"), lax.axis_index("gz")
    hh, hc = 1 - ix, ix
    top, bottom = ROWS - 1, ROWS + ny

    def wrap(i, n):
        return lax.rem(i + 2 * n, n)

    def order(i):
        return lax.rem(i + 1, nb)

    ring = 4 if nb > 4 else nb
    cols = nb // ring
    gx, gy = lax.div(g, ring), lax.rem(g, ring)

    def hops(o):
        dx, dy = o // ring, o % ring
        return min(dx, cols - dx) + min(dy, ring - dy)

    turns = sorted(range(nb), key=lambda o: (-hops(o), -min(o % ring, ring - o % ring), o))

    def turn(j):
        o = jnp.int32(turns[-1])
        for k in range(nb - 1):
            o = jnp.where(j == k, turns[k], o)
        return lax.div(o, ring), lax.rem(o, ring)

    def seen_from(col, row, step):
        return wrap(col + step[0], cols) * ring + wrap(row + step[1], ring)

    def rows8(b):
        return pl.ds(pl.multiple_of(ROWS * b, ROWS), ROWS)

    def shifted(b, by):
        return pl.ds(pl.multiple_of(ROWS * b, ROWS) + by, ROWS)

    def load(l, half):
        return pltpu.make_async_copy(
            f_ref.at[:, :, rows8(l), pl.ds(half * LANES, LANES)],
            vol.at[half, :, :, shifted(l, ROWS), :],
            load_sem.at[l],
        )

    def start_load(l, _):
        for half in range(2):
            load(l, half).start()
        return 0

    def landed(ref, sem):
        pltpu.make_async_copy(ref, ref, sem).wait()

    def wait_load(l):
        landed(vol.at[:, :, :, pl.ds(ROWS, ROWS), :], load_sem.at[l])

    barrier = pltpu.get_barrier_semaphore()

    def to_row(j):
        return {"gz": gx * ring + wrap(gy + j, ring)}

    def to_col(j):
        return {"gz": wrap(gx + j, cols) * ring + gy}

    def hello(sem, where):
        pl.semaphore_signal(sem, inc=1, device_id=where, device_id_type=MESH)

    skew_up = (gy == ring - 1) & (g < nb - 1)
    skew_down = (gy == 0) & (g > 0)

    hello(barrier, {"ix": 1 - ix})
    for there, where in (
        (iy > 0, {"iy": iy - 1}),
        (iy < n_iy - 1, {"iy": iy + 1}),
        (skew_up, {"gz": g + 1}),
        (skew_down, {"gz": g - 1}),
    ):
        @pl.when(there)
        def _(where=where):
            hello(barrier, where)
    for j in range(1, ring):
        hello(barrier, to_row(j))
    for j in range(1, cols):
        hello(barrier, to_col(j))
    beside = 1 + (ring - 1) + (cols - 1)
    for there in (iy > 0, iy < n_iy - 1, skew_up, skew_down):
        beside = beside + jnp.where(there, 1, 0)

    colors = pltpu.make_async_copy(p_ref, pal_ref, pal_sem)
    colors.start()
    lax.fori_loop(0, pair + 2, start_load, 0)
    lax.fori_loop(pair + 2, nb, start_load, 0)

    def y_copy(side, half, remote):
        source = 0 if remote == (side == 1) else ny - 1
        src = f_ref.at[:, :, pl.ds(source, 1), pl.ds(half * LANES, LANES)]
        dst = vol.at[half, :, :, pl.ds(bottom if side else top, 1), :]
        if not remote:
            return pltpu.make_async_copy(src, dst, yrecv.at[side])
        return pltpu.make_async_remote_copy(
            src, dst, ysend.at[side], yrecv.at[side],
            device_id={"iy": iy - 1 if side else iy + 1}, device_id_type=MESH,
        )

    def z_copy(side, b, remote):
        source = 0 if remote == (side == 1) else nz - 1
        src = f_ref.at[:, source, rows8(b), :]
        dst = zh.at[side, :, rows8(b), :]
        if not remote:
            return pltpu.make_async_copy(src, dst, zrecv.at[b])
        return pltpu.make_async_remote_copy(
            src, dst, zsend.at[side], zrecv.at[b],
            device_id={"gz": g - 1 if side else g + 1}, device_id_type=MESH,
        )

    up, down = [(lax.div(n, ring), lax.rem(n, ring)) for n in (g + 1, g + nb - 1)]

    def z_start(j, _):
        step = turn(j)

        @pl.when(g < nb - 1)
        def _():
            z_copy(0, seen_from(*up, step), True).start()

        @pl.when(g > 0)
        def _():
            z_copy(1, seen_from(*down, step), True).start()

        return 0

    def z_clamp(side):
        def one(b, _):
            z_copy(side, b, False).start()
            return 0

        lax.fori_loop(0, nb, one, 0)

    def y_start():
        for half in range(2):
            @pl.when(iy < n_iy - 1)
            def _():
                y_copy(0, half, True).start()

            @pl.when(iy > 0)
            def _():
                y_copy(1, half, True).start()

            @pl.when(iy == 0)
            def _():
                y_copy(0, half, False).start()

            @pl.when(iy == n_iy - 1)
            def _():
                y_copy(1, half, False).start()

    lane = lax.broadcasted_iota(jnp.int32, (ROWS, LANES), 1)
    out_roll = jnp.where(ix == 0, LANES - 1, 1)
    in_roll = LANES - out_roll
    edge = jnp.where(ix == 0, LANES - 1, 0)
    at_edge = lane == edge
    at_inner = lane == LANES - 1 - edge
    nz_dir = jnp.where(ix == 0, 0.45, -0.45).astype(F32)
    ny_dir = jnp.where(ix == 0, 0.6, -0.6).astype(F32)
    colors.wait()
    pal = [[0.5 * pal_ref[i, c] for c in range(3)] for i in range(2)]

    def spread(z, side):
        return 2 * z + 1 if z % 2 == 0 else 2 * z - 1 + side

    def pack(b, f, edges):
        side = jnp.where(ix == 0, -1, 1)
        acc = None
        for z in range(0, nz, 2):
            both = jnp.where(at_edge, edges[z][0], edges[z + 1][1])
            to = spread(z, side)
            both = pltpu.roll(both, lax.rem(to - edge + LANES, LANES), 1)
            acc = both if acc is None else jnp.where(lane >= to - 1, both, acc)
        hs[f, rows8(b), :] = acc

    def x_copy(b):
        return pltpu.make_async_remote_copy(
            hs.at[:, rows8(b), :], hx.at[:, rows8(b), :], xsend, xrecv.at[b],
            device_id={"ix": 1 - ix}, device_id_type=MESH,
        )

    def a_copy(b, slot):
        return pltpu.make_async_remote_copy(
            part.at[b], recv.at[slot], asend, arecv,
            device_id={"gz": b}, device_id_type=MESH,
        )

    def planes(b, f, z):
        return [vol[half, f, z, shifted(b, ROWS), :] for half in (hc, hh)]

    def at(half, f, z, b):
        return vol[half, f, z, shifted(b, ROWS), :]

    def dy_of(half, f, z, b):
        return vol[half, f, z, shifted(b, ROWS + 1), :] - vol[half, f, z, shifted(b, ROWS - 1), :]

    def beyond(side, f, half, b):
        return zh[side, f, rows8(b), pl.ds(pl.multiple_of(half * LANES, LANES), LANES)]

    def column(half, f, z, b):
        if z < 0:
            return beyond(0, f, half, b)
        if z >= nz:
            return beyond(1, f, half, b)
        return at(half, f, z, b)

    def dz_of(half, f, z, b):
        return column(half, f, z + 1, b) - column(half, f, z - 1, b)

    def inner_dx(f, z, b, now, out):
        inward = pltpu.roll(now, in_roll, 1)
        dx = jnp.where(at_edge, out, pltpu.roll(now, out_roll, 1)) - jnp.where(at_inner, now, inward)
        return dx, inward

    def outer_dx(f, z, b, now, out, inward):
        side = jnp.where(ix == 0, 1, -1)
        beside = pltpu.roll(hx[f, rows8(b), :], lax.rem(edge - spread(z, side) + LANES, LANES), 1)
        return jnp.where(at_edge, beside, out) - jnp.where(at_inner, inward, pltpu.roll(now, in_roll, 1))

    def shade(half, z, b, now, dx):
        dz = [dz_of(half, f, z, b) for f in range(2)]
        dy = [dy_of(half, f, z, b) for f in range(2)]
        return cell(
            dz[0], dy[0], dx[0], now[0], dz[1], dy[1], dx[1], now[1], pal, nz_dir, ny_dir
        )

    def clean():
        zero, one = jnp.zeros((ROWS, LANES), F32), jnp.ones((ROWS, LANES), F32)
        return [zero, one] + [zero] * 4

    def add(state, d, light, tints):
        depth = state[0] + d
        still = jnp.exp2(depth)
        lit = (state[1] - still) * light
        return [depth, still, state[2] + lit] + [state[3 + c] + lit * tints[c] for c in range(3)]

    def inner_half(blocks):
        states = [clean() for _ in blocks]
        edges = [[[] for _ in range(2)] for _ in blocks]
        for z in range(nz):
            for k, b in enumerate(blocks):
                now, dx = [], []
                for f in range(2):
                    h = at(hh, f, z, b)
                    out = pltpu.roll(h, out_roll, 1)
                    outs[f, z, rows8(b), :] = out
                    edges[k][f].append((h, out))
                    if 0 < z < cut:
                        now.append(at(hc, f, z, b))
                        d, inward = inner_dx(f, z, b, now[f], out)
                        ins[f, z, rows8(b), :] = inward
                        dx.append(d)
                if 0 < z < cut:
                    states[k] = add(states[k], *shade(hc, z, b, now, dx))
        for k, b in enumerate(blocks):
            for f in range(2):
                pack(b, f, edges[k][f])
            for c in range(6):
                inner[b, c] = states[k][c]

    def outer_half(blocks):
        fronts = [None for _ in blocks]
        backs = [clean() for _ in blocks]
        states = [clean() for _ in blocks]
        for z in range(nz):
            for k, b in enumerate(blocks):
                now = [at(hh, f, z, b) for f in range(2)]
                out = [outs[f, z, rows8(b), :] for f in range(2)]
                if 0 < z < cut:
                    inward = [ins[f, z, rows8(b), :] for f in range(2)]
                else:
                    mine = [at(hc, f, z, b) for f in range(2)]
                    pairs = [inner_dx(f, z, b, mine[f], out[f]) for f in range(2)]
                    inward = [p[1] for p in pairs]
                    shaded = shade(hc, z, b, mine, [p[0] for p in pairs])
                    if z == 0:
                        fronts[k] = add(clean(), *shaded)
                    else:
                        backs[k] = add(backs[k], *shaded)
                dx = [outer_dx(f, z, b, now[f], out[f], inward[f]) for f in range(2)]
                states[k] = add(states[k], *shade(hh, z, b, now, dx))
        for k, b in enumerate(blocks):
            keep(b, hh, states[k])
            front, back = fronts[k], backs[k]
            mid = [inner[b, c] for c in range(6)]
            keep(
                b, hc,
                [front[0] + mid[0] + back[0], None]
                + [front[c] + front[1] * (mid[c] + mid[1] * back[c]) for c in range(2, 6)],
            )

    def keep(b, half, state):
        to = pl.ds(pl.multiple_of(half * LANES, LANES), LANES)
        for c in range(3):
            part[b, c, :, to] = 1.12 * (state[2] + state[3 + c])
        part[b, 3, :, to] = state[0]

    def send(b):
        @pl.when(b != g)
        def _():
            a_copy(b, g).start()

    for l in range(2):
        wait_load(l)

    def enter():
        pl.semaphore_wait(barrier, beside)
        for j in range(1, cols):
            hello(all_sem, to_col(j))
        y_start()

        def columns(i, _):
            x_copy(order(i)).start()
            return 0

        lax.fori_loop(0, entry, columns, 0)
        lax.fori_loop(0, nb, z_start, 0)

        @pl.when(g == 0)
        def _():
            z_clamp(0)

        @pl.when(g == nb - 1)
        def _():
            z_clamp(1)

    def step(s, _):
        @pl.when(s == entry // pair)
        def _():
            enter()

        i = s * pair

        @pl.when(i < nb)
        def _():
            for k in range(pair):
                @pl.when(i + k + 2 < nb)
                def _():
                    wait_load(i + k + 2)

                for side, row in ((0, 0), (1, nb - 1)):
                    @pl.when(order(i + k) == row)
                    def _():
                        landed(vol.at[:, :, :, pl.ds(0, 1), :], yrecv.at[side])

            inner_half([order(i + k) for k in range(pair)])

            @pl.when(i >= entry)
            def _():
                for k in range(pair):
                    x_copy(order(i + k)).start()

        @pl.when(i == gap)
        def _():
            if cols > 1:
                pl.semaphore_wait(all_sem, cols - 1)

        @pl.when(i >= gap)
        def _():
            j = i - gap
            blocks = [seen_from(gx, gy, turn(j + k)) for k in range(pair)]
            for k in range(pair):
                x_copy(blocks[k]).wait_recv()
                landed(zh.at[:, :, rows8(blocks[k]), :], zrecv.at[blocks[k]])
            outer_half(blocks)
            for k in range(pair):
                send(blocks[k])

        return 0

    lax.fori_loop(0, (nb + gap) // pair, step, 0)
    recv[g] = part[g]
    landed(hs, xsend)

    @pl.when(g < nb - 1)
    def _():
        landed(zh.at[0], zsend.at[0])

    @pl.when(g > 0)
    def _():
        landed(zh.at[1], zsend.at[1])

    for side, there in ((0, iy < n_iy - 1), (1, iy > 0)):
        @pl.when(there)
        def _(side=side):
            landed(vol.at[:, :, :, pl.ds(0, 1), :], ysend.at[side])

    landed(part.at[pl.ds(0, nb - 1)], asend)
    landed(recv.at[pl.ds(0, nb - 1)], arecv)
    ahead = jnp.zeros(recv.shape[2:], F32)
    sums = [jnp.zeros(recv.shape[2:], F32) for _ in range(3)]
    for k in range(nb):
        clear = jnp.exp2(ahead)
        sums = [sums[c] + clear * recv[k, c] for c in range(3)]
        ahead = ahead + recv[k, 3]
    for c in range(3):
        o_ref[c] = sums[c]
    o_ref[3] = 1.0 - jnp.exp2(ahead)

def body(sizes, fields, palette):
    n_gz = sizes[2]
    _, nz, ny, nx = fields.shape
    gap, entry, pair = (16, 2, 1) if n_gz > 4 else (4, 1, 1)
    cut = nz - 12 if nz > 16 else nz - 3
    dma = pltpu.SemaphoreType.DMA
    return pl.pallas_call(
        functools.partial(kernel, sizes, gap, entry, pair, cut),
        out_shape=jax.ShapeDtypeStruct((4, ny // n_gz, nx), F32),
        in_specs=[
            pl.BlockSpec(memory_space=pl.ANY),
            pl.BlockSpec(memory_space=pl.ANY),
        ],
        out_specs=pl.BlockSpec(memory_space=pltpu.VMEM),
        scratch_shapes=[
            pltpu.SMEM((2, 3), F32),
            pltpu.VMEM((2, 2, nz, ny + 2 * ROWS, LANES), F32),
            pltpu.VMEM((2, 2, ny, nx), F32),
            pltpu.VMEM((2, ny, LANES), F32),
            pltpu.VMEM((2, ny, LANES), F32),
            pltpu.VMEM((2, nz, ny, LANES), F32),
            pltpu.VMEM((2, nz, ny, LANES), F32),
            pltpu.VMEM((n_gz, 6, ROWS, LANES), F32),
            pltpu.VMEM((n_gz, 4, ROWS, nx), F32),
            pltpu.VMEM((n_gz, 4, ROWS, nx), F32),
            dma(()),
            pltpu.SemaphoreType.REGULAR,
            dma((n_gz,)),
            dma((2,)),
            dma((n_gz,)),
            dma((2,)),
            dma((2,)),
            dma(()),
            dma((n_gz,)),
            dma(()),
            dma(()),
        ],
        compiler_params=pltpu.CompilerParams(
            collective_id=0, has_side_effects=True, vmem_limit_bytes=50 << 20
        ),
    )(palette, fields)

def solution(mesh):
    sizes = tuple(mesh.shape[axis] for axis in ("iy", "ix", "gz"))
    return jax.shard_map(
        functools.partial(body, sizes),
        mesh=mesh,
        in_specs=(P(None, "gz", "iy", "ix"), P()),
        out_specs=P(None, ("iy", "gz"), "ix"),
        check_vma=False,
    )
```

```python
import functools

import jax
import jax.numpy as jnp
from jax import lax
from jax.experimental import pallas as pl
from jax.experimental.pallas import tpu as pltpu
from jax.sharding import PartitionSpec as P

MESH = pl.DeviceIdType.MESH

F32 = jnp.float32
LANES = 128
ROWS = 8
LOG2E = 1.4426950408889634
C1 = 0.005 * LOG2E
C2 = 0.016 * LOG2E

def cell(dz, dy, dx, s, ez, ey, ex, u, pal, nz, ny):
    r = lax.rsqrt(dz * dz + dy * dy + dx * dx + 4.0)
    depth = jnp.exp2(s * LOG2E) * (C2 * (r * r) - C1)
    face = jnp.abs(nz * dz + ny * dy + dx) * r + 0.3 / 0.56
    around = pltpu.reciprocal(ez * ez + ey * ey + ex * ex + 4.0, approx=True)
    light = face * (0.375 - around)
    tints = [jnp.tanh(pal[0][c] * u + pal[1][c]) for c in range(3)]
    return depth, light, tints

def kernel(
    sizes, gap, entry, pair, cut,
    p_ref, f_ref, o_ref,
    pal_ref, vol, zh, hs, hx, outs, ins, inner, part, recv,
    pal_sem, all_sem, load_sem, zsend, zrecv, ysend, yrecv, xsend, xrecv, asend, arecv,
):
    n_iy, n_ix, n_gz = sizes
    nz, ny = f_ref.shape[1], f_ref.shape[2]
    nb = n_gz
    iy, ix, g = lax.axis_index("iy"), lax.axis_index("ix"), lax.axis_index("gz")
    hh, hc = 1 - ix, ix
    top, bottom = ROWS - 1, ROWS + ny

    def wrap(i, n):
        return lax.rem(i + 2 * n, n)

    def order(i):
        return lax.rem(i + 1, nb)

    ring = 4 if nb > 4 else nb
    cols = nb // ring
    gx, gy = lax.div(g, ring), lax.rem(g, ring)

    def hops(o):
        dx, dy = o // ring, o % ring
        return min(dx, cols - dx) + min(dy, ring - dy)

    turns = sorted(range(nb), key=lambda o: (-min(o % ring, ring - o % ring), -min(o // ring, cols - o // ring), o))

    def turn(j):
        o = jnp.int32(turns[-1])
        for k in range(nb - 1):
            o = jnp.where(j == k, turns[k], o)
        return lax.div(o, ring), lax.rem(o, ring)

    def seen_from(col, row, step):
        return wrap(col + step[0], cols) * ring + wrap(row + step[1], ring)

    def rows8(b):
        return pl.ds(pl.multiple_of(ROWS * b, ROWS), ROWS)

    def shifted(b, by):
        return pl.ds(pl.multiple_of(ROWS * b, ROWS) + by, ROWS)

    def load(l, half):
        return pltpu.make_async_copy(
            f_ref.at[:, :, rows8(l), pl.ds(half * LANES, LANES)],
            vol.at[half, :, :, shifted(l, ROWS), :],
            load_sem.at[l],
        )

    def start_load(l, _):
        for half in range(2):
            load(l, half).start()
        return 0

    def landed(ref, sem):
        pltpu.make_async_copy(ref, ref, sem).wait()

    def wait_load(l):
        landed(vol.at[:, :, :, pl.ds(ROWS, ROWS), :], load_sem.at[l])

    barrier = pltpu.get_barrier_semaphore()

    def to_row(j):
        return {"gz": gx * ring + wrap(gy + j, ring)}

    def to_col(j):
        return {"gz": wrap(gx + j, cols) * ring + gy}

    def hello(sem, where):
        pl.semaphore_signal(sem, inc=1, device_id=where, device_id_type=MESH)

    skew_up = (gy == ring - 1) & (g < nb - 1)
    skew_down = (gy == 0) & (g > 0)

    hello(barrier, {"ix": 1 - ix})
    for there, where in (
        (iy > 0, {"iy": iy - 1}),
        (iy < n_iy - 1, {"iy": iy + 1}),
        (skew_up, {"gz": g + 1}),
        (skew_down, {"gz": g - 1}),
    ):
        @pl.when(there)
        def _(where=where):
            hello(barrier, where)
    for j in range(1, ring):
        hello(barrier, to_row(j))
    for j in range(1, cols):
        hello(barrier, to_col(j))
    beside = 1 + (ring - 1) + (cols - 1)
    for there in (iy > 0, iy < n_iy - 1, skew_up, skew_down):
        beside = beside + jnp.where(there, 1, 0)

    colors = pltpu.make_async_copy(p_ref, pal_ref, pal_sem)
    colors.start()
    lax.fori_loop(0, pair + 2, start_load, 0)
    lax.fori_loop(pair + 2, nb, start_load, 0)

    def y_copy(side, half, remote):
        source = 0 if remote == (side == 1) else ny - 1
        src = f_ref.at[:, :, pl.ds(source, 1), pl.ds(half * LANES, LANES)]
        dst = vol.at[half, :, :, pl.ds(bottom if side else top, 1), :]
        if not remote:
            return pltpu.make_async_copy(src, dst, yrecv.at[side])
        return pltpu.make_async_remote_copy(
            src, dst, ysend.at[side], yrecv.at[side],
            device_id={"iy": iy - 1 if side else iy + 1}, device_id_type=MESH,
        )

    def z_copy(side, b, remote):
        source = 0 if remote == (side == 1) else nz - 1
        src = f_ref.at[:, source, rows8(b), :]
        dst = zh.at[side, :, rows8(b), :]
        if not remote:
            return pltpu.make_async_copy(src, dst, zrecv.at[b])
        return pltpu.make_async_remote_copy(
            src, dst, zsend.at[side], zrecv.at[b],
            device_id={"gz": g - 1 if side else g + 1}, device_id_type=MESH,
        )

    up, down = [(lax.div(n, ring), lax.rem(n, ring)) for n in (g + 1, g + nb - 1)]

    def z_start(j, _):
        step = turn(j)

        @pl.when(g < nb - 1)
        def _():
            z_copy(0, seen_from(*up, step), True).start()

        @pl.when(g > 0)
        def _():
            z_copy(1, seen_from(*down, step), True).start()

        return 0

    def z_clamp(side):
        def one(b, _):
            z_copy(side, b, False).start()
            return 0

        lax.fori_loop(0, nb, one, 0)

    def y_start():
        for half in range(2):
            @pl.when(iy < n_iy - 1)
            def _():
                y_copy(0, half, True).start()

            @pl.when(iy > 0)
            def _():
                y_copy(1, half, True).start()

            @pl.when(iy == 0)
            def _():
                y_copy(0, half, False).start()

            @pl.when(iy == n_iy - 1)
            def _():
                y_copy(1, half, False).start()

    lane = lax.broadcasted_iota(jnp.int32, (ROWS, LANES), 1)
    out_roll = jnp.where(ix == 0, LANES - 1, 1)
    in_roll = LANES - out_roll
    edge = jnp.where(ix == 0, LANES - 1, 0)
    at_edge = lane == edge
    at_inner = lane == LANES - 1 - edge
    nz_dir = jnp.where(ix == 0, 0.45, -0.45).astype(F32)
    ny_dir = jnp.where(ix == 0, 0.6, -0.6).astype(F32)
    colors.wait()
    pal = [[0.5 * pal_ref[i, c] for c in range(3)] for i in range(2)]

    def spread(z, side):
        return 2 * z + 1 if z % 2 == 0 else 2 * z - 1 + side

    def pack(b, f, edges):
        side = jnp.where(ix == 0, -1, 1)
        acc = None
        for z in range(0, nz, 2):
            both = jnp.where(at_edge, edges[z][0], edges[z + 1][1])
            to = spread(z, side)
            both = pltpu.roll(both, lax.rem(to - edge + LANES, LANES), 1)
            acc = both if acc is None else jnp.where(lane >= to - 1, both, acc)
        hs[f, rows8(b), :] = acc

    def x_copy(b):
        return pltpu.make_async_remote_copy(
            hs.at[:, rows8(b), :], hx.at[:, rows8(b), :], xsend, xrecv.at[b],
            device_id={"ix": 1 - ix}, device_id_type=MESH,
        )

    def a_copy(b, slot):
        return pltpu.make_async_remote_copy(
            part.at[b], recv.at[slot], asend, arecv,
            device_id={"gz": b}, device_id_type=MESH,
        )

    def planes(b, f, z):
        return [vol[half, f, z, shifted(b, ROWS), :] for half in (hc, hh)]

    def at(half, f, z, b):
        return vol[half, f, z, shifted(b, ROWS), :]

    def dy_of(half, f, z, b):
        return vol[half, f, z, shifted(b, ROWS + 1), :] - vol[half, f, z, shifted(b, ROWS - 1), :]

    def beyond(side, f, half, b):
        return zh[side, f, rows8(b), pl.ds(pl.multiple_of(half * LANES, LANES), LANES)]

    def column(half, f, z, b):
        if z < 0:
            return beyond(0, f, half, b)
        if z >= nz:
            return beyond(1, f, half, b)
        return at(half, f, z, b)

    def dz_of(half, f, z, b):
        return column(half, f, z + 1, b) - column(half, f, z - 1, b)

    def inner_dx(f, z, b, now, out):
        inward = pltpu.roll(now, in_roll, 1)
        dx = jnp.where(at_edge, out, pltpu.roll(now, out_roll, 1)) - jnp.where(at_inner, now, inward)
        return dx, inward

    def outer_dx(f, z, b, now, out, inward):
        side = jnp.where(ix == 0, 1, -1)
        beside = pltpu.roll(hx[f, rows8(b), :], lax.rem(edge - spread(z, side) + LANES, LANES), 1)
        return jnp.where(at_edge, beside, out) - jnp.where(at_inner, inward, pltpu.roll(now, in_roll, 1))

    def shade(half, z, b, now, dx):
        dz = [dz_of(half, f, z, b) for f in range(2)]
        dy = [dy_of(half, f, z, b) for f in range(2)]
        return cell(
            dz[0], dy[0], dx[0], now[0], dz[1], dy[1], dx[1], now[1], pal, nz_dir, ny_dir
        )

    def clean():
        zero, one = jnp.zeros((ROWS, LANES), F32), jnp.ones((ROWS, LANES), F32)
        return [zero, one] + [zero] * 4

    def add(state, d, light, tints):
        depth = state[0] + d
        still = jnp.exp2(depth)
        lit = (state[1] - still) * light
        return [depth, still, state[2] + lit] + [state[3 + c] + lit * tints[c] for c in range(3)]

    def inner_half(blocks):
        states = [clean() for _ in blocks]
        edges = [[[] for _ in range(2)] for _ in blocks]
        for z in range(nz):
            for k, b in enumerate(blocks):
                now, dx = [], []
                for f in range(2):
                    h = at(hh, f, z, b)
                    out = pltpu.roll(h, out_roll, 1)
                    outs[f, z, rows8(b), :] = out
                    edges[k][f].append((h, out))
                    if 0 < z < cut:
                        now.append(at(hc, f, z, b))
                        d, inward = inner_dx(f, z, b, now[f], out)
                        ins[f, z, rows8(b), :] = inward
                        dx.append(d)
                if 0 < z < cut:
                    states[k] = add(states[k], *shade(hc, z, b, now, dx))
        for k, b in enumerate(blocks):
            for f in range(2):
                pack(b, f, edges[k][f])
            for c in range(6):
                inner[b, c] = states[k][c]

    def outer_half(blocks):
        fronts = [None for _ in blocks]
        backs = [clean() for _ in blocks]
        states = [clean() for _ in blocks]
        for z in range(nz):
            for k, b in enumerate(blocks):
                now = [at(hh, f, z, b) for f in range(2)]
                out = [outs[f, z, rows8(b), :] for f in range(2)]
                if 0 < z < cut:
                    inward = [ins[f, z, rows8(b), :] for f in range(2)]
                else:
                    mine = [at(hc, f, z, b) for f in range(2)]
                    pairs = [inner_dx(f, z, b, mine[f], out[f]) for f in range(2)]
                    inward = [p[1] for p in pairs]
                    shaded = shade(hc, z, b, mine, [p[0] for p in pairs])
                    if z == 0:
                        fronts[k] = add(clean(), *shaded)
                    else:
                        backs[k] = add(backs[k], *shaded)
                dx = [outer_dx(f, z, b, now[f], out[f], inward[f]) for f in range(2)]
                states[k] = add(states[k], *shade(hh, z, b, now, dx))
        for k, b in enumerate(blocks):
            keep(b, hh, states[k])
            front, back = fronts[k], backs[k]
            mid = [inner[b, c] for c in range(6)]
            keep(
                b, hc,
                [front[0] + mid[0] + back[0], None]
                + [front[c] + front[1] * (mid[c] + mid[1] * back[c]) for c in range(2, 6)],
            )

    def keep(b, half, state):
        to = pl.ds(pl.multiple_of(half * LANES, LANES), LANES)
        for c in range(3):
            part[b, c, :, to] = 1.12 * (state[2] + state[3 + c])
        part[b, 3, :, to] = state[0]

    def send(b):
        @pl.when(b != g)
        def _():
            a_copy(b, g).start()

    for l in range(2):
        wait_load(l)

    def enter():
        pl.semaphore_wait(barrier, beside)
        for j in range(1, cols):
            hello(all_sem, to_col(j))
        y_start()

        def columns(i, _):
            x_copy(order(i)).start()
            return 0

        lax.fori_loop(0, entry, columns, 0)
        lax.fori_loop(0, nb, z_start, 0)

        @pl.when(g == 0)
        def _():
            z_clamp(0)

        @pl.when(g == nb - 1)
        def _():
            z_clamp(1)

    def step(s, _):
        @pl.when(s == entry // pair)
        def _():
            enter()

        i = s * pair

        @pl.when(i < nb)
        def _():
            for k in range(pair):
                @pl.when(i + k + 2 < nb)
                def _():
                    wait_load(i + k + 2)

                for side, row in ((0, 0), (1, nb - 1)):
                    @pl.when(order(i + k) == row)
                    def _():
                        landed(vol.at[:, :, :, pl.ds(0, 1), :], yrecv.at[side])

            inner_half([order(i + k) for k in range(pair)])

            @pl.when(i >= entry)
            def _():
                for k in range(pair):
                    x_copy(order(i + k)).start()

        @pl.when(i == gap)
        def _():
            if cols > 1:
                pl.semaphore_wait(all_sem, cols - 1)

        @pl.when(i >= gap)
        def _():
            j = i - gap
            blocks = [seen_from(gx, gy, turn(j + k)) for k in range(pair)]
            for k in range(pair):
                x_copy(blocks[k]).wait_recv()
                landed(zh.at[:, :, rows8(blocks[k]), :], zrecv.at[blocks[k]])
            outer_half(blocks)
            for k in range(pair):
                send(blocks[k])

        return 0

    lax.fori_loop(0, (nb + gap) // pair, step, 0)
    recv[g] = part[g]
    landed(hs, xsend)

    @pl.when(g < nb - 1)
    def _():
        landed(zh.at[0], zsend.at[0])

    @pl.when(g > 0)
    def _():
        landed(zh.at[1], zsend.at[1])

    for side, there in ((0, iy < n_iy - 1), (1, iy > 0)):
        @pl.when(there)
        def _(side=side):
            landed(vol.at[:, :, :, pl.ds(0, 1), :], ysend.at[side])

    landed(part.at[pl.ds(0, nb - 1)], asend)
    landed(recv.at[pl.ds(0, nb - 1)], arecv)
    ahead = jnp.zeros(recv.shape[2:], F32)
    sums = [jnp.zeros(recv.shape[2:], F32) for _ in range(3)]
    for k in range(nb):
        clear = jnp.exp2(ahead)
        sums = [sums[c] + clear * recv[k, c] for c in range(3)]
        ahead = ahead + recv[k, 3]
    for c in range(3):
        o_ref[c] = sums[c]
    o_ref[3] = 1.0 - jnp.exp2(ahead)

def body(sizes, fields, palette):
    n_gz = sizes[2]
    _, nz, ny, nx = fields.shape
    gap, entry, pair = (16, 2, 1) if n_gz > 4 else (4, 1, 1)
    cut = nz - 16 if nz > 16 else nz - 3
    dma = pltpu.SemaphoreType.DMA
    return pl.pallas_call(
        functools.partial(kernel, sizes, gap, entry, pair, cut),
        out_shape=jax.ShapeDtypeStruct((4, ny // n_gz, nx), F32),
        in_specs=[
            pl.BlockSpec(memory_space=pl.ANY),
            pl.BlockSpec(memory_space=pl.ANY),
        ],
        out_specs=pl.BlockSpec(memory_space=pltpu.VMEM),
        scratch_shapes=[
            pltpu.SMEM((2, 3), F32),
            pltpu.VMEM((2, 2, nz, ny + 2 * ROWS, LANES), F32),
            pltpu.VMEM((2, 2, ny, nx), F32),
            pltpu.VMEM((2, ny, LANES), F32),
            pltpu.VMEM((2, ny, LANES), F32),
            pltpu.VMEM((2, nz, ny, LANES), F32),
            pltpu.VMEM((2, nz, ny, LANES), F32),
            pltpu.VMEM((n_gz, 6, ROWS, LANES), F32),
            pltpu.VMEM((n_gz, 4, ROWS, nx), F32),
            pltpu.VMEM((n_gz, 4, ROWS, nx), F32),
            dma(()),
            pltpu.SemaphoreType.REGULAR,
            dma((n_gz,)),
            dma((2,)),
            dma((n_gz,)),
            dma((2,)),
            dma((2,)),
            dma(()),
            dma((n_gz,)),
            dma(()),
            dma(()),
        ],
        compiler_params=pltpu.CompilerParams(
            collective_id=0, has_side_effects=True, vmem_limit_bytes=50 << 20
        ),
    )(palette, fields)

def solution(mesh):
    sizes = tuple(mesh.shape[axis] for axis in ("iy", "ix", "gz"))
    return jax.shard_map(
        functools.partial(body, sizes),
        mesh=mesh,
        in_specs=(P(None, "gz", "iy", "ix"), P()),
        out_specs=P(None, ("iy", "gz"), "ix"),
        check_vma=False,
    )
```

```python
import functools

import jax
import jax.numpy as jnp
from jax import lax
from jax.experimental import pallas as pl
from jax.experimental.pallas import tpu as pltpu
from jax.sharding import PartitionSpec as P

MESH = pl.DeviceIdType.MESH

F32 = jnp.float32
LANES = 128
ROWS = 8
LOG2E = 1.4426950408889634
C1 = 0.005 * LOG2E
C2 = 0.016 * LOG2E

def cell(dz, dy, dx, s, ez, ey, ex, u, pal, nz, ny):
    r = lax.rsqrt(dz * dz + dy * dy + dx * dx + 4.0)
    depth = jnp.exp2(s * LOG2E) * (C2 * (r * r) - C1)
    face = jnp.abs(nz * dz + ny * dy + dx) * r + 0.3 / 0.56
    around = pltpu.reciprocal(ez * ez + ey * ey + ex * ex + 4.0, approx=True)
    light = face * (0.375 - around)
    tints = [jnp.tanh(pal[0][c] * u + pal[1][c]) for c in range(3)]
    return depth, light, tints

def kernel(
    sizes, gap, entry, pair, cut,
    p_ref, f_ref, o_ref,
    pal_ref, vol, zh, hs, hx, outs, ins, inner, part, recv,
    pal_sem, all_sem, load_sem, zsend, zrecv, ysend, yrecv, xsend, xrecv, asend, arecv,
):
    n_iy, n_ix, n_gz = sizes
    nz, ny = f_ref.shape[1], f_ref.shape[2]
    nb = n_gz
    iy, ix, g = lax.axis_index("iy"), lax.axis_index("ix"), lax.axis_index("gz")
    hh, hc = 1 - ix, ix
    top, bottom = ROWS - 1, ROWS + ny

    def wrap(i, n):
        return lax.rem(i + 2 * n, n)

    def order(i):
        return lax.rem(i + 1, nb)

    ring = 4 if nb > 4 else nb
    cols = nb // ring
    gx, gy = lax.div(g, ring), lax.rem(g, ring)

    def hops(o):
        dx, dy = o // ring, o % ring
        return min(dx, cols - dx) + min(dy, ring - dy)

    turns = sorted(range(nb), key=lambda o: (-min(o % ring, ring - o % ring), -min(o // ring, cols - o // ring), o))

    def turn(j):
        o = jnp.int32(turns[-1])
        for k in range(nb - 1):
            o = jnp.where(j == k, turns[k], o)
        return lax.div(o, ring), lax.rem(o, ring)

    def seen_from(col, row, step):
        return wrap(col + step[0], cols) * ring + wrap(row + step[1], ring)

    def rows8(b):
        return pl.ds(pl.multiple_of(ROWS * b, ROWS), ROWS)

    def shifted(b, by):
        return pl.ds(pl.multiple_of(ROWS * b, ROWS) + by, ROWS)

    def load(l, half):
        return pltpu.make_async_copy(
            f_ref.at[:, :, rows8(l), pl.ds(half * LANES, LANES)],
            vol.at[half, :, :, shifted(l, ROWS), :],
            load_sem.at[l],
        )

    def start_load(l, _):
        for half in range(2):
            load(l, half).start()
        return 0

    def landed(ref, sem):
        pltpu.make_async_copy(ref, ref, sem).wait()

    def wait_load(l):
        landed(vol.at[:, :, :, pl.ds(ROWS, ROWS), :], load_sem.at[l])

    barrier = pltpu.get_barrier_semaphore()

    def to_row(j):
        return {"gz": gx * ring + wrap(gy + j, ring)}

    def to_col(j):
        return {"gz": wrap(gx + j, cols) * ring + gy}

    def hello(sem, where):
        pl.semaphore_signal(sem, inc=1, device_id=where, device_id_type=MESH)

    skew_up = (gy == ring - 1) & (g < nb - 1)
    skew_down = (gy == 0) & (g > 0)

    hello(barrier, {"ix": 1 - ix})
    for there, where in (
        (iy > 0, {"iy": iy - 1}),
        (iy < n_iy - 1, {"iy": iy + 1}),
        (skew_up, {"gz": g + 1}),
        (skew_down, {"gz": g - 1}),
    ):
        @pl.when(there)
        def _(where=where):
            hello(barrier, where)
    for j in range(1, ring):
        hello(barrier, to_row(j))
    for j in range(1, cols):
        hello(barrier, to_col(j))
    beside = 1 + (ring - 1) + (cols - 1)
    for there in (iy > 0, iy < n_iy - 1, skew_up, skew_down):
        beside = beside + jnp.where(there, 1, 0)

    colors = pltpu.make_async_copy(p_ref, pal_ref, pal_sem)
    colors.start()
    lax.fori_loop(0, pair + 2, start_load, 0)
    lax.fori_loop(pair + 2, nb, start_load, 0)

    def y_copy(side, half, remote):
        source = 0 if remote == (side == 1) else ny - 1
        src = f_ref.at[:, :, pl.ds(source, 1), pl.ds(half * LANES, LANES)]
        dst = vol.at[half, :, :, pl.ds(bottom if side else top, 1), :]
        if not remote:
            return pltpu.make_async_copy(src, dst, yrecv.at[side])
        return pltpu.make_async_remote_copy(
            src, dst, ysend.at[side], yrecv.at[side],
            device_id={"iy": iy - 1 if side else iy + 1}, device_id_type=MESH,
        )

    def z_copy(side, b, remote):
        source = 0 if remote == (side == 1) else nz - 1
        src = f_ref.at[:, source, rows8(b), :]
        dst = zh.at[side, :, rows8(b), :]
        if not remote:
            return pltpu.make_async_copy(src, dst, zrecv.at[b])
        return pltpu.make_async_remote_copy(
            src, dst, zsend.at[side], zrecv.at[b],
            device_id={"gz": g - 1 if side else g + 1}, device_id_type=MESH,
        )

    up, down = [(lax.div(n, ring), lax.rem(n, ring)) for n in (g + 1, g + nb - 1)]

    def z_start(j, _):
        step = turn(j)

        @pl.when(g < nb - 1)
        def _():
            z_copy(0, seen_from(*up, step), True).start()

        @pl.when(g > 0)
        def _():
            z_copy(1, seen_from(*down, step), True).start()

        return 0

    def z_clamp(side):
        def one(b, _):
            z_copy(side, b, False).start()
            return 0

        lax.fori_loop(0, nb, one, 0)

    def y_start():
        for half in range(2):
            @pl.when(iy < n_iy - 1)
            def _():
                y_copy(0, half, True).start()

            @pl.when(iy > 0)
            def _():
                y_copy(1, half, True).start()

            @pl.when(iy == 0)
            def _():
                y_copy(0, half, False).start()

            @pl.when(iy == n_iy - 1)
            def _():
                y_copy(1, half, False).start()

    lane = lax.broadcasted_iota(jnp.int32, (ROWS, LANES), 1)
    out_roll = jnp.where(ix == 0, LANES - 1, 1)
    in_roll = LANES - out_roll
    edge = jnp.where(ix == 0, LANES - 1, 0)
    at_edge = lane == edge
    at_inner = lane == LANES - 1 - edge
    nz_dir = jnp.where(ix == 0, 0.45, -0.45).astype(F32)
    ny_dir = jnp.where(ix == 0, 0.6, -0.6).astype(F32)
    colors.wait()
    pal = [[0.5 * pal_ref[i, c] for c in range(3)] for i in range(2)]

    def spread(z, side):
        return 2 * z + 1 if z % 2 == 0 else 2 * z - 1 + side

    def pack(b, f, edges):
        side = jnp.where(ix == 0, -1, 1)
        acc = None
        for z in range(0, nz, 2):
            both = jnp.where(at_edge, edges[z][0], edges[z + 1][1])
            to = spread(z, side)
            both = pltpu.roll(both, lax.rem(to - edge + LANES, LANES), 1)
            acc = both if acc is None else jnp.where(lane >= to - 1, both, acc)
        hs[f, rows8(b), :] = acc

    def x_copy(b):
        return pltpu.make_async_remote_copy(
            hs.at[:, rows8(b), :], hx.at[:, rows8(b), :], xsend, xrecv.at[b],
            device_id={"ix": 1 - ix}, device_id_type=MESH,
        )

    def a_copy(b, slot):
        return pltpu.make_async_remote_copy(
            part.at[b], recv.at[slot], asend, arecv,
            device_id={"gz": b}, device_id_type=MESH,
        )

    def planes(b, f, z):
        return [vol[half, f, z, shifted(b, ROWS), :] for half in (hc, hh)]

    def at(half, f, z, b):
        return vol[half, f, z, shifted(b, ROWS), :]

    def dy_of(half, f, z, b):
        return vol[half, f, z, shifted(b, ROWS + 1), :] - vol[half, f, z, shifted(b, ROWS - 1), :]

    def beyond(side, f, half, b):
        return zh[side, f, rows8(b), pl.ds(pl.multiple_of(half * LANES, LANES), LANES)]

    def column(half, f, z, b):
        if z < 0:
            return beyond(0, f, half, b)
        if z >= nz:
            return beyond(1, f, half, b)
        return at(half, f, z, b)

    def dz_of(half, f, z, b):
        return column(half, f, z + 1, b) - column(half, f, z - 1, b)

    def inner_dx(f, z, b, now, out):
        inward = pltpu.roll(now, in_roll, 1)
        dx = jnp.where(at_edge, out, pltpu.roll(now, out_roll, 1)) - jnp.where(at_inner, now, inward)
        return dx, inward

    def outer_dx(f, z, b, now, out, inward):
        side = jnp.where(ix == 0, 1, -1)
        beside = pltpu.roll(hx[f, rows8(b), :], lax.rem(edge - spread(z, side) + LANES, LANES), 1)
        return jnp.where(at_edge, beside, out) - jnp.where(at_inner, inward, pltpu.roll(now, in_roll, 1))

    def shade(half, z, b, now, dx):
        dz = [dz_of(half, f, z, b) for f in range(2)]
        dy = [dy_of(half, f, z, b) for f in range(2)]
        return cell(
            dz[0], dy[0], dx[0], now[0], dz[1], dy[1], dx[1], now[1], pal, nz_dir, ny_dir
        )

    def clean():
        zero, one = jnp.zeros((ROWS, LANES), F32), jnp.ones((ROWS, LANES), F32)
        return [zero, one] + [zero] * 4

    def add(state, d, light, tints):
        depth = state[0] + d
        still = jnp.exp2(depth)
        lit = (state[1] - still) * light
        return [depth, still, state[2] + lit] + [state[3 + c] + lit * tints[c] for c in range(3)]

    def inner_half(blocks):
        states = [clean() for _ in blocks]
        edges = [[[] for _ in range(2)] for _ in blocks]
        for z in range(nz):
            for k, b in enumerate(blocks):
                now, dx = [], []
                for f in range(2):
                    h = at(hh, f, z, b)
                    out = pltpu.roll(h, out_roll, 1)
                    outs[f, z, rows8(b), :] = out
                    edges[k][f].append((h, out))
                    if 0 < z < cut:
                        now.append(at(hc, f, z, b))
                        d, inward = inner_dx(f, z, b, now[f], out)
                        ins[f, z, rows8(b), :] = inward
                        dx.append(d)
                if 0 < z < cut:
                    states[k] = add(states[k], *shade(hc, z, b, now, dx))
        for k, b in enumerate(blocks):
            for f in range(2):
                pack(b, f, edges[k][f])
            for c in range(6):
                inner[b, c] = states[k][c]

    def outer_half(blocks):
        fronts = [None for _ in blocks]
        backs = [clean() for _ in blocks]
        states = [clean() for _ in blocks]
        for z in range(nz):
            for k, b in enumerate(blocks):
                now = [at(hh, f, z, b) for f in range(2)]
                out = [outs[f, z, rows8(b), :] for f in range(2)]
                if 0 < z < cut:
                    inward = [ins[f, z, rows8(b), :] for f in range(2)]
                else:
                    mine = [at(hc, f, z, b) for f in range(2)]
                    pairs = [inner_dx(f, z, b, mine[f], out[f]) for f in range(2)]
                    inward = [p[1] for p in pairs]
                    shaded = shade(hc, z, b, mine, [p[0] for p in pairs])
                    if z == 0:
                        fronts[k] = add(clean(), *shaded)
                    else:
                        backs[k] = add(backs[k], *shaded)
                dx = [outer_dx(f, z, b, now[f], out[f], inward[f]) for f in range(2)]
                states[k] = add(states[k], *shade(hh, z, b, now, dx))
        for k, b in enumerate(blocks):
            keep(b, hh, states[k])
            front, back = fronts[k], backs[k]
            mid = [inner[b, c] for c in range(6)]
            keep(
                b, hc,
                [front[0] + mid[0] + back[0], None]
                + [front[c] + front[1] * (mid[c] + mid[1] * back[c]) for c in range(2, 6)],
            )

    def keep(b, half, state):
        to = pl.ds(pl.multiple_of(half * LANES, LANES), LANES)
        for c in range(3):
            part[b, c, :, to] = 1.12 * (state[2] + state[3 + c])
        part[b, 3, :, to] = state[0]

    def send(b):
        @pl.when(b != g)
        def _():
            a_copy(b, g).start()

    for l in range(2):
        wait_load(l)

    def enter():
        pl.semaphore_wait(barrier, beside)
        for j in range(1, cols):
            hello(all_sem, to_col(j))
        y_start()

        def columns(i, _):
            x_copy(order(i)).start()
            return 0

        lax.fori_loop(0, entry, columns, 0)
        lax.fori_loop(0, nb, z_start, 0)

        @pl.when(g == 0)
        def _():
            z_clamp(0)

        @pl.when(g == nb - 1)
        def _():
            z_clamp(1)

    def step(s, _):
        @pl.when(s == entry // pair)
        def _():
            enter()

        i = s * pair

        @pl.when(i < nb)
        def _():
            for k in range(pair):
                @pl.when(i + k + 2 < nb)
                def _():
                    wait_load(i + k + 2)

                for side, row in ((0, 0), (1, nb - 1)):
                    @pl.when(order(i + k) == row)
                    def _():
                        landed(vol.at[:, :, :, pl.ds(0, 1), :], yrecv.at[side])

            inner_half([order(i + k) for k in range(pair)])

            @pl.when(i >= entry)
            def _():
                for k in range(pair):
                    x_copy(order(i + k)).start()

        @pl.when(i == gap)
        def _():
            if cols > 1:
                pl.semaphore_wait(all_sem, cols - 1)

        @pl.when(i >= gap)
        def _():
            j = i - gap
            blocks = [seen_from(gx, gy, turn(j + k)) for k in range(pair)]
            for k in range(pair):
                x_copy(blocks[k]).wait_recv()
                landed(zh.at[:, :, rows8(blocks[k]), :], zrecv.at[blocks[k]])
            outer_half(blocks)
            for k in range(pair):
                send(blocks[k])

        return 0

    lax.fori_loop(0, (nb + gap) // pair, step, 0)
    landed(hs, xsend)

    @pl.when(g < nb - 1)
    def _():
        landed(zh.at[0], zsend.at[0])

    @pl.when(g > 0)
    def _():
        landed(zh.at[1], zsend.at[1])

    for side, there in ((0, iy < n_iy - 1), (1, iy > 0)):
        @pl.when(there)
        def _(side=side):
            landed(vol.at[:, :, :, pl.ds(0, 1), :], ysend.at[side])

    recv[g] = part[g]
    landed(recv.at[pl.ds(0, nb - 1)], arecv)
    ahead = jnp.zeros(recv.shape[2:], F32)
    sums = [jnp.zeros(recv.shape[2:], F32) for _ in range(3)]
    for k in range(nb):
        clear = jnp.exp2(ahead)
        sums = [sums[c] + clear * recv[k, c] for c in range(3)]
        ahead = ahead + recv[k, 3]
    for c in range(3):
        o_ref[c] = sums[c]
    o_ref[3] = 1.0 - jnp.exp2(ahead)
    landed(part.at[pl.ds(0, nb - 1)], asend)

def body(sizes, fields, palette):
    n_gz = sizes[2]
    _, nz, ny, nx = fields.shape
    gap, entry, pair = (16, 2, 1) if n_gz > 4 else (4, 1, 1)
    cut = nz - 16 if nz > 16 else nz - 3
    dma = pltpu.SemaphoreType.DMA
    return pl.pallas_call(
        functools.partial(kernel, sizes, gap, entry, pair, cut),
        out_shape=jax.ShapeDtypeStruct((4, ny // n_gz, nx), F32),
        in_specs=[
            pl.BlockSpec(memory_space=pl.ANY),
            pl.BlockSpec(memory_space=pl.ANY),
        ],
        out_specs=pl.BlockSpec(memory_space=pltpu.VMEM),
        scratch_shapes=[
            pltpu.SMEM((2, 3), F32),
            pltpu.VMEM((2, 2, nz, ny + 2 * ROWS, LANES), F32),
            pltpu.VMEM((2, 2, ny, nx), F32),
            pltpu.VMEM((2, ny, LANES), F32),
            pltpu.VMEM((2, ny, LANES), F32),
            pltpu.VMEM((2, nz, ny, LANES), F32),
            pltpu.VMEM((2, nz, ny, LANES), F32),
            pltpu.VMEM((n_gz, 6, ROWS, LANES), F32),
            pltpu.VMEM((n_gz, 4, ROWS, nx), F32),
            pltpu.VMEM((n_gz, 4, ROWS, nx), F32),
            dma(()),
            pltpu.SemaphoreType.REGULAR,
            dma((n_gz,)),
            dma((2,)),
            dma((n_gz,)),
            dma((2,)),
            dma((2,)),
            dma(()),
            dma((n_gz,)),
            dma(()),
            dma(()),
        ],
        compiler_params=pltpu.CompilerParams(
            collective_id=0, has_side_effects=True, vmem_limit_bytes=50 << 20
        ),
    )(palette, fields)

def solution(mesh):
    sizes = tuple(mesh.shape[axis] for axis in ("iy", "ix", "gz"))
    return jax.shard_map(
        functools.partial(body, sizes),
        mesh=mesh,
        in_specs=(P(None, "gz", "iy", "ix"), P()),
        out_specs=P(None, ("iy", "gz"), "ix"),
        check_vma=False,
    )
```
